256 devices in a mesh: bin: 4 (over x_lo, core), row: 64 (over z, x_hi, y).
Axes of the slice: x: 4 (x_hi: 2, x_lo: 2; x = x_hi * 2 + x_lo), y: 4, z: 8, core: 2. Of those that a mesh axis runs over, the one named last changes fastest.
Arguments:
- focusing: bfloat16 [12, 2, 4096, 4096], P('bin', None, 'row'), may hold values from -0.0625 to 0.0625
- snapshots: bfloat16 [12, 2, 4096, 128], P('bin', None, 'row'), may hold values from -6 to 6
Outputs:
- spectrum: float32 [2, 4096, 4096], P(None, 'row', 'bin')
The draws below stay inside these ranges and needn't reach their ends.
All inputs are finite; a program needn't handle non-finite values.
Results may differ from the reference program's by a relative error of at most 0.0034.
Values may be sent and summed in bfloat16 or wider, within the bound.
A program may use at most 64 MiB of HBM per device.

```python
import jax
import jax.numpy as jnp
from jax import lax

M = 4096
K = 128
BINS = 12


def block_levels(stream_key, shape, shards, low, top_value):
    gain = 1.0
    for axis_at, parts in shards:
        draws = jax.random.uniform(jax.random.fold_in(jax.random.fold_in(stream_key, 6), axis_at), (parts,), jnp.float32, low / len(shards), top_value / len(shards))
        gain = gain * jnp.repeat(jnp.exp(draws), shape[axis_at] // parts).reshape((-1,) + (1,) * (len(shape) - 1 - axis_at))
    return gain


def centred(rng, extent, spread, bound, pieces=(), held_as=jnp.bfloat16):
    entries = spread * jax.random.normal(rng, extent, jnp.float32)
    if pieces:
        entries = entries * block_levels(rng, extent, pieces, -0.22, 0.18)
    return jnp.clip(entries, -bound, bound).astype(held_as)


def setup_inputs(seed: int = 0) -> dict:
    keys = jax.random.split(jax.random.key(seed), 3)
    focusing = centred(keys[0], (BINS, 2, M, M), (2 * M) ** -0.5, 0.0625, ((0, 4), (2, 64)))
    snapshots = centred(keys[1], (BINS, 2, M, K), 1.0, 6.0, ((0, 4), (2, 64)))
    return {"focusing": focusing, "snapshots": snapshots}


def contract(left, right):
    return lax.dot_general(left, right, (((1,), (1,)), ((), ())), preferred_element_type=jnp.float32)


def reference(focusing, snapshots):
    total_real = jnp.zeros((M, M), jnp.float32)
    total_imag = jnp.zeros((M, M), jnp.float32)
    for index in range(BINS):
        t_real = focusing[index, 0]
        t_imag = focusing[index, 1]
        x_real = snapshots[index, 0]
        x_imag = snapshots[index, 1]
        y_real = (jnp.dot(t_real, x_real, preferred_element_type=jnp.float32) - jnp.dot(t_imag, x_imag, preferred_element_type=jnp.float32)).astype(jnp.bfloat16)
        y_imag = (jnp.dot(t_real, x_imag, preferred_element_type=jnp.float32) + jnp.dot(t_imag, x_real, preferred_element_type=jnp.float32)).astype(jnp.bfloat16)
        total_real = total_real + contract(y_real, y_real) + contract(y_imag, y_imag)
        total_imag = total_imag + contract(y_imag, y_real) - contract(y_real, y_imag)
    scale = 1.0 / (BINS * K)
    return jnp.stack([total_real, total_imag]) * scale
```

```python
import functools

import jax
import jax.numpy as jnp
from jax import lax
from jax.experimental import pallas as pl
from jax.experimental.pallas import tpu as pltpu
from jax.sharding import PartitionSpec as P

MESH = pl.DeviceIdType.MESH
BF16 = jnp.bfloat16
F32 = jnp.float32

SPLIT = (
    {"X": (0, 32), "Y": (32, 16), "Z": (48, 16)},
    {"X": (0, 16), "Y": (16, 32), "Z": (48, 16)},
    {"X": (0, 16), "Y": (16, 16), "Z": (32, 32)},
)
GAP = 3
N_COPIES = 256


def dot_t(left, right):
    return lax.dot_general(left, right, (((1,), (1,)), ((), ())), preferred_element_type=F32)


def kernel(scale, foc, snap, out, T, X, yrow, ycol, G, gin, S, R, tsem, ssem, rsem):
    b = lax.axis_index("bin")
    row = lax.axis_index("row")
    xl, c = b // 2, b % 2
    z, xh, y = row // 8, (row // 4) % 2, row % 4

    def at(dz=0, dx=0, dy=0):
        return (b, ((z + dz) % 8) * 8 + ((xh + dx) % 2) * 4 + (y + dy) % 4)

    loads = [pltpu.make_async_copy(foc.at[k], T.at[k], tsem.at[k]) for k in range(3)]
    for k in range(3):
        loads[k].start()

    partners = [at(dz=d) for d in range(1, 8)]
    for dl in range(2):
        for dx in range(2):
            for dy in range(4):
                if dl or dx or dy:
                    partners.append((((xl + dl) % 2) * 2 + c, z * 8 + ((xh + dx) % 2) * 4 + (y + dy) % 4))
    sibling = (xl * 2 + 1 - c, row)
    partners.append(sibling)
    barrier = pltpu.get_barrier_semaphore()
    for peer in partners:
        pl.semaphore_signal(barrier, inc=1, device_id=peer, device_id_type=MESH)

    for k in range(3):
        X[k, z, xh, y] = jnp.concatenate([snap[k, 0], snap[k, 1]], axis=1)

    pl.semaphore_wait(barrier, len(partners))

    count = [0]
    sent = []

    def send(src, dst, landing, peer):
        i = count[0]
        count[0] += 1
        copy = pltpu.make_async_remote_copy(
            src_ref=src, dst_ref=dst, send_sem=ssem.at[i], recv_sem=rsem.at[i], device_id=peer, device_id_type=MESH
        )
        copy.start()
        sent.append(copy)
        arrival = pltpu.make_async_remote_copy(
            src_ref=landing, dst_ref=landing, send_sem=ssem.at[i], recv_sem=rsem.at[i], device_id=peer, device_id_type=MESH
        )
        return arrival.wait_recv

    def wait_all(waits):
        for w in waits:
            w()

    def bin_steps(k):
        rx, ry, rz = (pl.ds(*SPLIT[k][t]) for t in "XYZ")
        w = {}

        def zfirst(name, rs):
            own = X.at[k, z, xh, y, rs]
            w[name] = [send(own, own, X.at[k, (z + 8 - d) % 8, xh, y, rs], at(dz=d)) for d in (4, 3, 5, 2, 6, 1, 7)]

        def s0():
            own = X.at[k, z, xh, y, rz]
            w["Z1"] = [send(own, own, X.at[k, z, 1 - xh, y, rz], at(dx=1))]
            zfirst("X1", rx)
            zfirst("Y1", ry)

        def s1():
            wait_all(w["Z1"])
            own = X.at[k, z, :, y, rz]
            w["Z2"] = [send(own, own, X.at[k, z, :, (y + 4 - d) % 4, rz], at(dy=d)) for d in (2, 1, 3)]
            wait_all(w["X1"])
            own = X.at[k, :, xh, y, rx]
            w["X2"] = [send(own, own, X.at[k, :, xh, (y + 4 - d) % 4, rx], at(dy=d)) for d in (2, 1, 3)]
            wait_all(w["Y1"])
            own = X.at[k, :, xh, y, ry]
            w["Y2"] = [send(own, own, X.at[k, :, 1 - xh, y, ry], at(dx=1))]

        def zring(far, halves_up, halves_down):
            up = [None, None]
            down = [None, None]
            for h in halves_up:
                piece = X.at[k, (z + 8 - far) % 8, h, :, rz]
                up[h] = send(piece, piece, X.at[k, (z + 8 - far - 1) % 8, h, :, rz], at(dz=1))
            for h in halves_down:
                piece = X.at[k, (z + far) % 8, h, :, rz]
                down[h] = send(piece, piece, X.at[k, (z + far + 1) % 8, h, :, rz], at(dz=7))
            return up, down

        def forward(far):
            up0, down0 = w["ring"]
            up, down = [None, None], [None, None]
            for h in range(2):
                up0[h]()
                if far < 3 or h == 0:
                    piece = X.at[k, (z + 8 - far) % 8, h, :, rz]
                    up[h] = send(piece, piece, X.at[k, (z + 8 - far - 1) % 8, h, :, rz], at(dz=1))
                down0[h]()
                if far < 3 or h == 1:
                    piece = X.at[k, (z + far) % 8, h, :, rz]
                    down[h] = send(piece, piece, X.at[k, (z + far + 1) % 8, h, :, rz], at(dz=7))
            w["ring"] = up, down

        def s2():
            wait_all(w["Z2"])
            w["ring"] = zring(0, (0, 1), (0, 1))
            wait_all(w["Y2"])
            own = X.at[k, :, :, y, ry]
            w["Y3"] = [send(own, own, X.at[k, :, :, (y + 4 - d) % 4, ry], at(dy=d)) for d in (1, 3)]
            wait_all(w["X2"])
            own = X.at[k, :, xh, :, rx]
            w["X3"] = [send(own, own, X.at[k, :, 1 - xh, :, rx], at(dx=1))]

        def s3():
            forward(1)
            w["Y3"][0]()
            piece = X.at[k, :, 0, (y + 3) % 4, ry]
            up = send(piece, piece, X.at[k, :, 0, (y + 2) % 4, ry], at(dy=1))
            w["Y3"][1]()
            piece = X.at[k, :, 1, (y + 1) % 4, ry]
            down = send(piece, piece, X.at[k, :, 1, (y + 2) % 4, ry], at(dy=3))
            w["Y4"] = [up, down]

        def s4():
            forward(2)

        def s5():
            forward(3)

        def s6():
            up, down = w["ring"]
            up[0]()
            down[1]()
            wait_all(w["Y4"])
            wait_all(w["X3"])
            loads[k].wait()

            def plane(i, acc):
                cols = pl.ds(pl.multiple_of(i * 512, 512), 512)
                return acc + jnp.dot(
                    T[k, :, :, cols].reshape(128, 512), X[k, i].reshape(512, 256), preferred_element_type=F32
                )

            acc = lax.fori_loop(0, 8, plane, jnp.zeros((128, 256), F32))
            real = acc[:64, :128] - acc[64:, 128:]
            imag = acc[:64, 128:] + acc[64:, :128]
            focused = jnp.concatenate([real, imag], axis=1).astype(BF16)
            yrow[k, xh, y] = focused
            ycol[k, z] = focused
            own = ycol.at[k, z]
            w["C"] = [send(own, own, ycol.at[k, (z + 8 - d) % 8], at(dz=d)) for d in (4, 3, 5, 2, 6, 1, 7)]
            own = yrow.at[k, xh, y]
            w["R"] = [
                send(own, own, yrow.at[k, (xh + dx) % 2, (y + 4 - dy) % 4], at(dx=dx, dy=dy))
                for dx, dy in ((1, 2), (1, 1), (1, 3), (1, 0), (0, 2), (0, 1), (0, 3))
            ]

        def s7():
            wait_all(w["C"])
            wait_all(w["R"])
            if k < 2:
                for part in range(2):
                    for half in range(2):
                        gram(k, part, half)

        return [s0, s1, s2, s3, s4, s5, s6, s7]

    def gram(k, part, half):
        left = yrow[k, half].reshape(256, 256)
        right = jnp.concatenate(
            [ycol[k, pl.ds(2 * part, 2)].reshape(128, 256), ycol[k, pl.ds(4 + 2 * part, 2)].reshape(128, 256)], axis=0
        )
        turned = jnp.concatenate([-right[:, 128:], right[:, :128]], axis=1)
        if k == 0:
            G[part, half, 0] = dot_t(left, right)
            G[part, half, 1] = dot_t(left, turned)
        else:
            G[part, half, 0] += dot_t(left, right)
            G[part, half, 1] += dot_t(left, turned)

    events = []
    for k in range(3):
        for i, step in enumerate(bin_steps(k)):
            events.append((k * GAP + i, -i, k, step))
    for e in sorted(events, key=lambda e: e[:3]):
        e[3]()

    waits = []
    for half in ((xh + 1) % 2, xh):
        gram(2, 1 - c, half)
        piece = G.at[1 - c, half]
        waits.append(send(piece, gin.at[half], gin.at[half], sibling))
    final = []
    for n, half in enumerate(((xh + 1) % 2, xh)):
        gram(2, c, half)
        waits[n]()
        total = (G[c, half] + gin[half]) * scale
        for part in range(2):
            S[part, half] = total[:, :, part * 128 : (part + 1) * 128].reshape(2, 4, 64, 128).astype(BF16)
        dx = 1 - n
        for dl, dy in ((1, 2), (1, 1), (1, 3), (0, 2), (0, 1), (0, 3), (1, 0), (0, 0)):
            if dl or dx or dy:
                to_l, to_x, to_y = (xl + dl) % 2, (xh + dx) % 2, (y + dy) % 4
                final.append(
                    send(
                        S.at[to_l, to_x, :, to_y],
                        R.at[xl, xh, y],
                        R.at[(xl + dl) % 2, (xh + dx) % 2, (y + 4 - dy) % 4],
                        (to_l * 2 + c, z * 8 + to_x * 4 + to_y),
                    )
                )
    R[xl, xh, y] = S[xl, xh, :, y]
    wait_all(final)
    for zi in range(2):
        for h in range(2):
            for yp in range(2):
                lanes = slice(zi * 64, zi * 64 + 64)
                pair = [
                    R[0, h, 2 * yp + o].astype(F32) + R[1, h, 2 * yp + o].astype(F32) for o in range(2)
                ]
                out[:, :, zi * 512 + h * 256 + yp * 128 : zi * 512 + h * 256 + yp * 128 + 128] = jnp.concatenate(
                    [pair[0][:, :, lanes], pair[1][:, :, lanes]], axis=2
                )
    for copy in sent:
        copy.wait_send()


def on_device(focusing, snapshots):
    scale = 1.0 / (12 * 128)
    return pl.pallas_call(
        functools.partial(kernel, scale),
        out_shape=jax.ShapeDtypeStruct((2, 64, 1024), F32),
        in_specs=[pl.BlockSpec(memory_space=pl.ANY), pl.BlockSpec(memory_space=pltpu.VMEM)],
        out_specs=pl.BlockSpec(memory_space=pltpu.VMEM),
        scratch_shapes=[
            pltpu.VMEM((3, 2, 64, 4096), BF16),
            pltpu.VMEM((3, 8, 2, 4, 64, 256), BF16),
            pltpu.VMEM((3, 2, 4, 64, 256), BF16),
            pltpu.VMEM((3, 8, 64, 256), BF16),
            pltpu.VMEM((2, 2, 2, 256, 256), F32),
            pltpu.VMEM((2, 2, 256, 256), F32),
            pltpu.VMEM((2, 2, 2, 4, 64, 128), BF16),
            pltpu.VMEM((2, 2, 4, 2, 64, 128), BF16),
            pltpu.SemaphoreType.DMA((3,)),
            pltpu.SemaphoreType.DMA((N_COPIES,)),
            pltpu.SemaphoreType.DMA((N_COPIES,)),
        ],
        compiler_params=pltpu.CompilerParams(
            collective_id=0, has_side_effects=True, vmem_limit_bytes=48 * 2**20
        ),
        name="focus_gram",
    )(focusing, snapshots)


def solution(mesh):
    placed = (P("bin", None, "row", None), P("bin", None, "row", None))
    return jax.shard_map(
        on_device, mesh=mesh, in_specs=placed, out_specs=P(None, "row", "bin"), check_vma=False
    )
```

```python
import functools

import jax
import jax.numpy as jnp
from jax import lax
from jax.experimental import pallas as pl
from jax.experimental.pallas import tpu as pltpu
from jax.sharding import PartitionSpec as P

MESH = pl.DeviceIdType.MESH
BF16 = jnp.bfloat16
F32 = jnp.float32

PIECES = (
    (0, "X", 0, 32), (0, "Y", 32, 32),
    (1, "X", 0, 32), (1, "Y", 32, 32),
    (2, "Z", 0, 64),
)
ORDER = (0, 1, 2)
WHEN = {
    "X": {0: (0.2, 5, 12), 1: (0.4, 9, 18)},
    "Y": {0: (0.1, 4.5, 9, 16, 20), 1: (0.3, 8.5, 12, 19, 25)},
    "Z": {2: (0, 3, 6, 11, 16, 21)},
}
DONE = {0: 30, 1: 36, 2: 40}
GRAM = {0: 41, 1: 42, 2: 50}
N_COPIES = 256


def dot_t(left, right):
    return lax.dot_general(left, right, (((1,), (1,)), ((), ())), preferred_element_type=F32)


def kernel(scale, foc, snap_hbm, out, snap, T, X, yrow, ycol, G, gin, S, R, tsem, ssem, rsem):
    b = lax.axis_index("bin")
    row = lax.axis_index("row")
    xl, c = b // 2, b % 2
    z, xh, y = row // 8, (row // 4) % 2, row % 4

    def at(dz=0, dx=0, dy=0):
        return (b, ((z + dz) % 8) * 8 + ((xh + dx) % 2) * 4 + (y + dy) % 4)

    fetch = pltpu.make_async_copy(snap_hbm, snap, tsem.at[3])
    fetch.start()
    loads = [pltpu.make_async_copy(foc.at[k], T.at[k], tsem.at[k]) for k in range(3)]
    for k in range(3):
        loads[k].start()

    partners = [at(dz=d) for d in range(1, 8)]
    for dl in range(2):
        for dx in range(2):
            for dy in range(4):
                if dl or dx or dy:
                    partners.append((((xl + dl) % 2) * 2 + c, z * 8 + ((xh + dx) % 2) * 4 + (y + dy) % 4))
    sibling = (xl * 2 + 1 - c, row)
    partners.append(sibling)
    barrier = pltpu.get_barrier_semaphore()
    for peer in partners:
        pl.semaphore_signal(barrier, inc=1, device_id=peer, device_id_type=MESH)

    fetch.wait()
    for k in range(3):
        X[k, z, xh, y] = jnp.concatenate([snap[k, 0], snap[k, 1]], axis=1)

    pl.semaphore_wait(barrier, len(partners))

    count = [0]
    sent = []

    def send(src, dst, landing, peer):
        i = count[0]
        count[0] += 1
        copy = pltpu.make_async_remote_copy(
            src_ref=src, dst_ref=dst, send_sem=ssem.at[i], recv_sem=rsem.at[i], device_id=peer, device_id_type=MESH
        )
        copy.start()
        sent.append(copy)
        arrival = pltpu.make_async_remote_copy(
            src_ref=landing, dst_ref=landing, send_sem=ssem.at[i], recv_sem=rsem.at[i], device_id=peer, device_id_type=MESH
        )
        return arrival.wait_recv

    def wait_all(waits):
        for w in waits:
            w()

    events = []
    pending = {k: [] for k in range(3)}

    def event(when, step):
        events.append((when, len(events), step))

    def z_direct(k, rs):
        own = X.at[k, z, xh, y, rs]
        return [send(own, own, X.at[k, (z + 8 - d) % 8, xh, y, rs], at(dz=d)) for d in (4, 3, 5, 2, 6, 1, 7)]

    def order_x(k, rs, when):
        w = {}

        def to_x(dy):
            own = X.at[k, :, xh, (y + 4 - dy) % 4, rs]
            pending[k].append(send(own, own, X.at[k, :, 1 - xh, (y + 4 - dy) % 4, rs], at(dx=1)))

        def first():
            w["z"] = z_direct(k, rs)

        def second():
            wait_all(w["z"])
            own = X.at[k, :, xh, y, rs]
            w["y"] = [send(own, own, X.at[k, :, xh, (y + 4 - d) % 4, rs], at(dy=d)) for d in (1, 3, 2)]
            to_x(0)

        def third():
            for n, d in enumerate((1, 3, 2)):
                w["y"][n]()
                to_x(d)

        for t, step in zip(when, (first, second, third)):
            event(t, step)

    def order_y(k, rs, when):
        w = {}
        low, high = pl.ds(0, 4), pl.ds(4, 4)

        def to_y(h):
            own = X.at[k, :, h, y, rs]
            return [send(own, own, X.at[k, :, h, (y + 4 - d) % 4, rs], at(dy=d)) for d in (1, 3)]

        def on_y(h, arrivals):
            arrivals[0]()
            piece = X.at[k, low, h, (y + 3) % 4, rs]
            pending[k].append(send(piece, piece, X.at[k, low, h, (y + 2) % 4, rs], at(dy=1)))
            arrivals[1]()
            piece = X.at[k, high, h, (y + 1) % 4, rs]
            pending[k].append(send(piece, piece, X.at[k, high, h, (y + 2) % 4, rs], at(dy=3)))

        def first():
            w["z"] = z_direct(k, rs)

        def second():
            wait_all(w["z"])
            own = X.at[k, :, xh, y, rs]
            w["x"] = send(own, own, X.at[k, :, 1 - xh, y, rs], at(dx=1))
            w["a"] = to_y(xh)

        def third():
            w["x"]()
            w["b"] = to_y(1 - xh)

        def fourth():
            on_y(xh, w["a"])

        def fifth():
            on_y(1 - xh, w["b"])

        for t, step in zip(when, (first, second, third, fourth, fifth)):
            event(t, step)

    def order_z(k, rs, when):
        w = {}
        ring = {}

        def pass_on(far, d):
            line = (y + 4 - d) % 4
            if far < 4:
                if far:
                    ring[d][0]()
                h = pl.ds(0, 2) if far < 3 else pl.ds(0, 1)
                piece = X.at[k, (z + 8 - far) % 8, h, line, rs]
                up = send(piece, piece, X.at[k, (z + 7 - far) % 8, h, line, rs], at(dz=1))
                if far:
                    ring[d][1]()
                h = pl.ds(0, 2) if far < 3 else pl.ds(1, 1)
                piece = X.at[k, (z + far) % 8, h, line, rs]
                down = send(piece, piece, X.at[k, (z + far + 1) % 8, h, line, rs], at(dz=7))
                ring[d] = (up, down)
                if far == 3:
                    pending[k].extend((up, down))

        def first():
            own = X.at[k, z, xh, y, rs]
            w["x"] = send(own, own, X.at[k, z, 1 - xh, y, rs], at(dx=1))

        def second():
            w["x"]()
            own = X.at[k, z, :, y, rs]
            w["y"] = [send(own, own, X.at[k, z, :, (y + 4 - d) % 4, rs], at(dy=d)) for d in (1, 3, 2)]
            pass_on(0, 0)

        def third():
            for n, d in enumerate((1, 3, 2)):
                w["y"][n]()
                pass_on(0, d)

        def later(far):
            for d in (0, 1, 3, 2):
                pass_on(far, d)

        for t, step in zip(when, (first, second, third)):
            event(t, step)
        for far in range(1, 4):
            event(when[2 + far], functools.partial(later, far))

    def done(k):
        w = gathers[k] = []
        wait_all(pending[k])
        loads[k].wait()

        def plane(i, acc):
            cols = pl.ds(pl.multiple_of(i * 512, 512), 512)
            return acc + jnp.dot(
                T[k, :, :, cols].reshape(128, 512), X[k, i].reshape(512, 256), preferred_element_type=F32
            )

        acc = lax.fori_loop(0, 8, plane, jnp.zeros((128, 256), F32))
        real = acc[:64, :128] - acc[64:, 128:]
        imag = acc[:64, 128:] + acc[64:, :128]
        focused = jnp.concatenate([real, imag], axis=1).astype(BF16)
        yrow[k, xh, y] = focused
        ycol[k, z] = focused
        own = ycol.at[k, z]
        for d in (4, 3, 5, 2, 6, 1, 7):
            w.append(send(own, own, ycol.at[k, (z + 8 - d) % 8], at(dz=d)))
        own = yrow.at[k, xh, y]
        for dx, dy in ((1, 2), (1, 1), (1, 3), (1, 0), (0, 2), (0, 1), (0, 3)):
            w.append(send(own, own, yrow.at[k, (xh + dx) % 2, (y + 4 - dy) % 4], at(dx=dx, dy=dy)))

    def gathered(k):
        wait_all(gathers[k])
        if k != ORDER[2]:
            for part in range(2):
                for half in range(2):
                    gram(k, part, half)

    gathers = {}
    def gram(k, part, half):
        left = yrow[k, half].reshape(256, 256)
        right = jnp.concatenate(
            [ycol[k, pl.ds(2 * part, 2)].reshape(128, 256), ycol[k, pl.ds(4 + 2 * part, 2)].reshape(128, 256)], axis=0
        )
        turned = jnp.concatenate([-right[:, 128:], right[:, :128]], axis=1)
        if k == ORDER[0]:
            G[part, half, 0] = dot_t(left, right)
            G[part, half, 1] = dot_t(left, turned)
        else:
            G[part, half, 0] += dot_t(left, right)
            G[part, half, 1] += dot_t(left, turned)

    for k, kind, first_row, rows in PIECES:
        make = {"X": order_x, "Y": order_y, "Z": order_z}[kind]
        make(k, pl.ds(first_row, rows), WHEN[kind][k])
    for k in ORDER:
        event(DONE[k], functools.partial(done, k))
        event(GRAM[k], functools.partial(gathered, k))
    for e in sorted(events, key=lambda e: e[:2]):
        e[2]()

    waits = []
    for half in ((xh + 1) % 2, xh):
        gram(ORDER[2], 1 - c, half)
        piece = G.at[1 - c, half]
        waits.append(send(piece, gin.at[half], gin.at[half], sibling))
    final = []
    for n, half in enumerate(((xh + 1) % 2, xh)):
        gram(ORDER[2], c, half)
        waits[n]()
        total = (G[c, half] + gin[half]) * scale
        for part in range(2):
            S[part, half] = total[:, :, part * 128 : (part + 1) * 128].reshape(2, 4, 64, 128).astype(BF16)
        dx = 1 - n
        for dl, dy in ((1, 2), (1, 1), (1, 3), (0, 2), (0, 1), (0, 3), (1, 0), (0, 0)):
            if dl or dx or dy:
                to_l, to_x, to_y = (xl + dl) % 2, (xh + dx) % 2, (y + dy) % 4
                final.append(
                    send(
                        S.at[to_l, to_x, :, to_y],
                        R.at[xl, xh, y],
                        R.at[(xl + dl) % 2, (xh + dx) % 2, (y + 4 - dy) % 4],
                        (to_l * 2 + c, z * 8 + to_x * 4 + to_y),
                    )
                )
    R[xl, xh, y] = S[xl, xh, :, y]
    wait_all(final)
    for zi in range(2):
        for h in range(2):
            for yp in range(2):
                lanes = slice(zi * 64, zi * 64 + 64)
                pair = [
                    R[0, h, 2 * yp + o].astype(F32) + R[1, h, 2 * yp + o].astype(F32) for o in range(2)
                ]
                out[:, :, zi * 512 + h * 256 + yp * 128 : zi * 512 + h * 256 + yp * 128 + 128] = jnp.concatenate(
                    [pair[0][:, :, lanes], pair[1][:, :, lanes]], axis=2
                )
    for copy in sent:
        copy.wait_send()


def on_device(focusing, snapshots):
    scale = 1.0 / (12 * 128)
    return pl.pallas_call(
        functools.partial(kernel, scale),
        out_shape=jax.ShapeDtypeStruct((2, 64, 1024), F32),
        in_specs=[pl.BlockSpec(memory_space=pl.ANY)] * 2,
        out_specs=pl.BlockSpec(memory_space=pltpu.VMEM),
        scratch_shapes=[
            pltpu.VMEM((3, 2, 64, 128), BF16),
            pltpu.VMEM((3, 2, 64, 4096), BF16),
            pltpu.VMEM((3, 8, 2, 4, 64, 256), BF16),
            pltpu.VMEM((3, 2, 4, 64, 256), BF16),
            pltpu.VMEM((3, 8, 64, 256), BF16),
            pltpu.VMEM((2, 2, 2, 256, 256), F32),
            pltpu.VMEM((2, 2, 256, 256), F32),
            pltpu.VMEM((2, 2, 2, 4, 64, 128), BF16),
            pltpu.VMEM((2, 2, 4, 2, 64, 128), BF16),
            pltpu.SemaphoreType.DMA((4,)),
            pltpu.SemaphoreType.DMA((N_COPIES,)),
            pltpu.SemaphoreType.DMA((N_COPIES,)),
        ],
        compiler_params=pltpu.CompilerParams(
            collective_id=0, has_side_effects=True, vmem_limit_bytes=63 * 2**20
        ),
        name="focus_gram",
    )(focusing, snapshots)


def solution(mesh):
    placed = (P("bin", None, "row", None), P("bin", None, "row", None))
    return jax.shard_map(
        on_device, mesh=mesh, in_specs=placed, out_specs=P(None, "row", "bin"), check_vma=False
    )
```

```python
import functools

import jax
import jax.numpy as jnp
from jax import lax
from jax.experimental import pallas as pl
from jax.experimental.pallas import tpu as pltpu
from jax.sharding import PartitionSpec as P

MESH = pl.DeviceIdType.MESH
BF16 = jnp.bfloat16
F32 = jnp.float32

PIECES = (
    (0, "X", 0, 32), (0, "Y", 32, 32),
    (1, "X", 0, 32), (1, "Y", 32, 32),
    (2, "Z", 0, 64),
)
ORDER = (2, 0, 1)
WHEN = {
    "X": {0: (0.2, 5, 12), 1: (0.4, 9, 18)},
    "Y": {0: (0.1, 4.5, 9, 16, 20), 1: (0.3, 8.5, 12, 19, 25)},
    "Z": {2: (0, 3, 6, 11, 16, 21)},
}
DONE = {2: 26, 0: 30, 1: 40}
ROWS = {2: 41, 0: 42, 1: 44}
GRAM = {2: 45.5, 0: 45.7, 1: 50}
N_COPIES = 256


def dot_t(left, right):
    return lax.dot_general(left, right, (((1,), (1,)), ((), ())), preferred_element_type=F32)


def kernel(scale, foc, snap_hbm, out, snap, T, X, yrow, ycol, G, S, R, tsem, ssem, rsem):
    b = lax.axis_index("bin")
    row = lax.axis_index("row")
    xl, c = b // 2, b % 2
    z, xh, y = row // 8, (row // 4) % 2, row % 4

    def at(dz=0, dx=0, dy=0):
        return (b, ((z + dz) % 8) * 8 + ((xh + dx) % 2) * 4 + (y + dy) % 4)

    fetch = pltpu.make_async_copy(snap_hbm, snap, tsem.at[3])
    fetch.start()
    loads = [pltpu.make_async_copy(foc.at[k], T.at[k], tsem.at[k]) for k in range(3)]
    for k in range(3):
        loads[k].start()

    partners = [at(dz=d) for d in range(1, 8)]
    for dl in range(2):
        for dx in range(2):
            for dy in range(4):
                if dl or dx or dy:
                    partners.append((((xl + dl) % 2) * 2 + c, z * 8 + ((xh + dx) % 2) * 4 + (y + dy) % 4))
    sibling = (xl * 2 + 1 - c, row)
    partners.append(sibling)
    barrier = pltpu.get_barrier_semaphore()
    for peer in partners:
        pl.semaphore_signal(barrier, inc=1, device_id=peer, device_id_type=MESH)

    fetch.wait()
    for k in range(3):
        X[k, z, xh, y] = jnp.concatenate([snap[k, 0], snap[k, 1]], axis=1)

    pl.semaphore_wait(barrier, len(partners))

    count = [0]
    sent = []

    def send(src, dst, landing, peer):
        i = count[0]
        count[0] += 1
        copy = pltpu.make_async_remote_copy(
            src_ref=src, dst_ref=dst, send_sem=ssem.at[i], recv_sem=rsem.at[i], device_id=peer, device_id_type=MESH
        )
        copy.start()
        sent.append(copy)
        arrival = pltpu.make_async_remote_copy(
            src_ref=landing, dst_ref=landing, send_sem=ssem.at[i], recv_sem=rsem.at[i], device_id=peer, device_id_type=MESH
        )
        return arrival.wait_recv

    def wait_all(waits):
        for w in waits:
            w()

    events = []
    pending = {k: [] for k in range(3)}

    def event(when, step):
        events.append((when, len(events), step))

    def z_direct(k, rs):
        own = X.at[k, z, xh, y, rs]
        return [send(own, own, X.at[k, (z + 8 - d) % 8, xh, y, rs], at(dz=d)) for d in (4, 3, 5, 2, 6, 1, 7)]

    def order_x(k, rs, when):
        w = {}

        def to_x(dy):
            own = X.at[k, :, xh, (y + 4 - dy) % 4, rs]
            pending[k].append(send(own, own, X.at[k, :, 1 - xh, (y + 4 - dy) % 4, rs], at(dx=1)))

        def first():
            w["z"] = z_direct(k, rs)

        def second():
            wait_all(w["z"])
            own = X.at[k, :, xh, y, rs]
            w["y"] = [send(own, own, X.at[k, :, xh, (y + 4 - d) % 4, rs], at(dy=d)) for d in (1, 3, 2)]
            to_x(0)

        def third():
            for n, d in enumerate((1, 3, 2)):
                w["y"][n]()
                to_x(d)

        for t, step in zip(when, (first, second, third)):
            event(t, step)

    def order_y(k, rs, when):
        w = {}
        low, high = pl.ds(0, 4), pl.ds(4, 4)

        def to_y(h):
            own = X.at[k, :, h, y, rs]
            return [send(own, own, X.at[k, :, h, (y + 4 - d) % 4, rs], at(dy=d)) for d in (1, 3)]

        def on_y(h, arrivals):
            arrivals[0]()
            piece = X.at[k, low, h, (y + 3) % 4, rs]
            pending[k].append(send(piece, piece, X.at[k, low, h, (y + 2) % 4, rs], at(dy=1)))
            arrivals[1]()
            piece = X.at[k, high, h, (y + 1) % 4, rs]
            pending[k].append(send(piece, piece, X.at[k, high, h, (y + 2) % 4, rs], at(dy=3)))

        def first():
            w["z"] = z_direct(k, rs)

        def second():
            wait_all(w["z"])
            own = X.at[k, :, xh, y, rs]
            w["x"] = send(own, own, X.at[k, :, 1 - xh, y, rs], at(dx=1))
            w["a"] = to_y(xh)

        def third():
            w["x"]()
            w["b"] = to_y(1 - xh)

        def fourth():
            on_y(xh, w["a"])

        def fifth():
            on_y(1 - xh, w["b"])

        for t, step in zip(when, (first, second, third, fourth, fifth)):
            event(t, step)

    def order_z(k, rs, when):
        w = {}
        ring = {}

        def pass_on(far, d):
            line = (y + 4 - d) % 4
            if far < 4:
                if far:
                    ring[d][0]()
                h = pl.ds(0, 2) if far < 3 else pl.ds(0, 1)
                piece = X.at[k, (z + 8 - far) % 8, h, line, rs]
                up = send(piece, piece, X.at[k, (z + 7 - far) % 8, h, line, rs], at(dz=1))
                if far:
                    ring[d][1]()
                h = pl.ds(0, 2) if far < 3 else pl.ds(1, 1)
                piece = X.at[k, (z + far) % 8, h, line, rs]
                down = send(piece, piece, X.at[k, (z + far + 1) % 8, h, line, rs], at(dz=7))
                ring[d] = (up, down)
                if far == 3:
                    pending[k].extend((up, down))

        def first():
            own = X.at[k, z, xh, y, rs]
            w["x"] = send(own, own, X.at[k, z, 1 - xh, y, rs], at(dx=1))

        def second():
            w["x"]()
            own = X.at[k, z, :, y, rs]
            w["y"] = [send(own, own, X.at[k, z, :, (y + 4 - d) % 4, rs], at(dy=d)) for d in (1, 3, 2)]
            pass_on(0, 0)

        def third():
            for n, d in enumerate((1, 3, 2)):
                w["y"][n]()
                pass_on(0, d)

        def later(far):
            for d in (0, 1, 3, 2):
                pass_on(far, d)

        for t, step in zip(when, (first, second, third)):
            event(t, step)
        for far in range(1, 4):
            event(when[2 + far], functools.partial(later, far))

    def done(k):
        wait_all(pending[k])
        loads[k].wait()

        def plane(i, acc):
            cols = pl.ds(pl.multiple_of(i * 512, 512), 512)
            return acc + jnp.dot(
                T[k, :, :, cols].reshape(128, 512), X[k, i].reshape(512, 256), preferred_element_type=F32
            )

        acc = lax.fori_loop(0, 8, plane, jnp.zeros((128, 256), F32))
        real = acc[:64, :128] - acc[64:, 128:]
        imag = acc[:64, 128:] + acc[64:, :128]
        focused = jnp.concatenate([real, imag], axis=1).astype(BF16)
        yrow[k, 0, xh, y] = focused
        own = yrow.at[k, 0, xh, y]
        side, slot = (z // 2) % 2, (z // 4) * 2 + z % 2
        base = count[0]
        count[0] += 8
        place, landed = ycol.at[k, c, slot], rsem.at[base + slot * 2 + c]
        for n, d in enumerate((4, 3, 5, 2, 6, 1, 7)):
            copy = pltpu.make_async_remote_copy(
                src_ref=own, dst_ref=place, send_sem=ssem.at[base + n], recv_sem=landed,
                device_id=(xl * 2 + side, at(dz=d)[1]), device_id_type=MESH,
            )
            copy.start()
            sent.append(copy)
        copy = pltpu.make_async_remote_copy(
            src_ref=own, dst_ref=place, send_sem=ssem.at[base + 7], recv_sem=landed,
            device_id=sibling, device_id_type=MESH,
        )
        pl.when(side != c)(copy.start)
        to_sibling.append((side != c, copy))
        pl.when(side == c)(pltpu.make_async_copy(own, place, landed).start)
        columns[k] = [
            pltpu.make_async_copy(ycol.at[k, s, j], ycol.at[k, s, j], rsem.at[base + j * 2 + s]).wait
            for j in range(4)
            for s in range(2)
        ]
        own = yrow.at[k, 0, xh, y]
        rows[k] = [
            send(own, own, yrow.at[k, 0, (xh + dx) % 2, (y + 4 - dy) % 4], at(dx=dx, dy=dy))
            for dx, dy in ((1, 2), (1, 1), (1, 3), (1, 0), (0, 2), (0, 1), (0, 3))
        ]

    def rows_here(k):
        wait_all(rows[k])
        shared[k] = [send(yrow.at[k, 0], yrow.at[k, 1], yrow.at[k, 1], sibling)]

    def gram_both(k):
        wait_all(shared[k])
        wait_all(columns[k])
        mine, other = ycol[k, c].reshape(256, 256), ycol[k, 1 - c].reshape(256, 256)
        right = jnp.concatenate([mine, other], axis=1)
        turned = jnp.concatenate([-mine[:, 128:], mine[:, :128], -other[:, 128:], other[:, :128]], axis=1)
        for half in range(2):
            left = jnp.concatenate([yrow[k, s, half].reshape(256, 256) for s in range(2)], axis=1)
            if k == ORDER[0]:
                G[half, 0] = dot_t(left, right)
                G[half, 1] = dot_t(left, turned)
            else:
                G[half, 0] += dot_t(left, right)
                G[half, 1] += dot_t(left, turned)

    rows, columns, shared, to_sibling = {}, {}, {}, []
    for k, kind, first_row, n_rows in PIECES:
        make = {"X": order_x, "Y": order_y, "Z": order_z}[kind]
        make(k, pl.ds(first_row, n_rows), WHEN[kind][k])
    for k in ORDER:
        event(DONE[k], functools.partial(done, k))
        event(ROWS[k], functools.partial(rows_here, k))
        event(GRAM[k], functools.partial(gram_both, k))
    for e in sorted(events, key=lambda e: e[:2]):
        e[2]()

    final = []
    for n, half in enumerate(((xh + 1) % 2, xh)):
        total = G[half] * scale
        for part in range(2):
            S[part, half] = total[:, :, part * 128 : (part + 1) * 128].reshape(2, 4, 64, 128).astype(BF16)
        dx = 1 - n
        for dl, dy in ((1, 2), (1, 1), (1, 3), (0, 2), (0, 1), (0, 3), (1, 0), (0, 0)):
            if dl or dx or dy:
                to_l, to_x, to_y = (xl + dl) % 2, (xh + dx) % 2, (y + dy) % 4
                final.append(
                    send(
                        S.at[to_l, to_x, :, to_y],
                        R.at[xl, xh, y],
                        R.at[(xl + dl) % 2, (xh + dx) % 2, (y + 4 - dy) % 4],
                        (to_l * 2 + c, z * 8 + to_x * 4 + to_y),
                    )
                )
    R[xl, xh, y] = S[xl, xh, :, y]
    wait_all(final)
    for zi in range(2):
        for h in range(2):
            for yp in range(2):
                lanes = slice(zi * 64, zi * 64 + 64)
                pair = [
                    R[0, h, 2 * yp + o].astype(F32) + R[1, h, 2 * yp + o].astype(F32) for o in range(2)
                ]
                out[:, :, zi * 512 + h * 256 + yp * 128 : zi * 512 + h * 256 + yp * 128 + 128] = jnp.concatenate(
                    [pair[0][:, :, lanes], pair[1][:, :, lanes]], axis=2
                )
    for copy in sent:
        copy.wait_send()
    for started, copy in to_sibling:
        pl.when(started)(copy.wait_send)


def on_device(focusing, snapshots):
    scale = 1.0 / (12 * 128)
    return pl.pallas_call(
        functools.partial(kernel, scale),
        out_shape=jax.ShapeDtypeStruct((2, 64, 1024), F32),
        in_specs=[pl.BlockSpec(memory_space=pl.ANY)] * 2,
        out_specs=pl.BlockSpec(memory_space=pltpu.VMEM),
        scratch_shapes=[
            pltpu.VMEM((3, 2, 64, 128), BF16),
            pltpu.VMEM((3, 2, 64, 4096), BF16),
            pltpu.VMEM((3, 8, 2, 4, 64, 256), BF16),
            pltpu.VMEM((3, 2, 2, 4, 64, 256), BF16),
            pltpu.VMEM((3, 2, 4, 64, 256), BF16),
            pltpu.VMEM((2, 2, 256, 256), F32),
            pltpu.VMEM((2, 2, 2, 4, 64, 128), BF16),
            pltpu.VMEM((2, 2, 4, 2, 64, 128), BF16),
            pltpu.SemaphoreType.DMA((4,)),
            pltpu.SemaphoreType.DMA((N_COPIES,)),
            pltpu.SemaphoreType.DMA((N_COPIES,)),
        ],
        compiler_params=pltpu.CompilerParams(
            collective_id=0, has_side_effects=True, vmem_limit_bytes=63 * 2**20
        ),
        name="focus_gram",
    )(focusing, snapshots)


def solution(mesh):
    placed = (P("bin", None, "row", None), P("bin", None, "row", None))
    return jax.shard_map(
        on_device, mesh=mesh, in_specs=placed, out_specs=P(None, "row", "bin"), check_vma=False
    )
```

```python
import functools

import jax
import jax.numpy as jnp
from jax import lax
from jax.experimental import pallas as pl
from jax.experimental.pallas import tpu as pltpu
from jax.sharding import PartitionSpec as P

MESH = pl.DeviceIdType.MESH
BF16 = jnp.bfloat16
F32 = jnp.float32

PIECES = (("Z", 0, 64),)
WHEN = {"X": (0.5, 8, 15), "Z": (0, 3, 6, 11, 16, 21)}
SHARED = ((0, 32), (32, 32))
SHARED_WHEN = ((0.1, 3.1, 5, 0.5, 12, 9), (0.2, 3.2, 6.8, 0.5, 13, 9.5))
SWAP_WHEN = (3.3, 3.4, 6.1, 6.2)
DONE_2, ROWS_2, GRAM_2 = 36, 44, 50
DONE_M, ROWS_M, GRAM_M = 30, 40, 45
N_COPIES = 288
NEAR_FIRST = (1, 7, 2, 6, 3, 5, 4)


def dot_t(left, right):
    return lax.dot_general(left, right, (((1,), (1,)), ((), ())), preferred_element_type=F32)


def kernel(scale, foc, snap_hbm, out, snap, T, given, X, yrow, ycol, G, S, R, tsem, ssem, rsem):
    b = lax.axis_index("bin")
    row = lax.axis_index("row")
    xl, c = b // 2, b % 2
    z, xh, y = row // 8, (row // 4) % 2, row % 4
    mine = 1 - ((y + 1) // 2) % 2
    first_y = (y // 2) * 2
    swap_y = first_y * 2 + 1 - y

    def at(dz=0, dx=0, dy=0):
        return (b, ((z + dz) % 8) * 8 + ((xh + dx) % 2) * 4 + (y + dy) % 4)

    fetch = pltpu.make_async_copy(snap_hbm, snap, tsem.at[3])
    fetch.start()
    loads = [
        pltpu.make_async_copy(foc.at[mine], T.at[0], tsem.at[0]),
        pltpu.make_async_copy(foc.at[2], T.at[2], tsem.at[2]),
    ]
    for load in loads:
        load.start()

    partners = [at(dz=d) for d in range(1, 8)]
    for dl in range(2):
        for dx in range(2):
            for dy in range(4):
                if dl or dx or dy:
                    partners.append((((xl + dl) % 2) * 2 + c, z * 8 + ((xh + dx) % 2) * 4 + (y + dy) % 4))
    sibling = (xl * 2 + 1 - c, row)
    partners.append(sibling)
    barrier = pltpu.get_barrier_semaphore()
    for peer in partners:
        pl.semaphore_signal(barrier, inc=1, device_id=peer, device_id_type=MESH)

    fetch.wait()
    X[0, z, xh, y] = jnp.concatenate([snap[mine, 0], snap[mine, 1]], axis=1)
    X[2, z, xh, y] = jnp.concatenate([snap[2, 0], snap[2, 1]], axis=1)
    given[...] = jnp.concatenate([snap[1 - mine, 0], snap[1 - mine, 1]], axis=1)

    pl.semaphore_wait(barrier, len(partners))

    count = [0]
    sent = []

    def send(src, dst, landing, peer):
        i = count[0]
        count[0] += 1
        copy = pltpu.make_async_remote_copy(
            src_ref=src, dst_ref=dst, send_sem=ssem.at[i], recv_sem=rsem.at[i], device_id=peer, device_id_type=MESH
        )
        copy.start()
        sent.append(copy)
        arrival = pltpu.make_async_remote_copy(
            src_ref=landing, dst_ref=landing, send_sem=ssem.at[i], recv_sem=rsem.at[i], device_id=peer, device_id_type=MESH
        )
        return arrival.wait_recv

    def wait_all(waits):
        for w in waits:
            w()

    events = []
    pending = {0: [], 2: []}

    def event(when, step):
        events.append((when, len(events), step))

    def z_direct(k, rs):
        own = X.at[k, z, xh, y, rs]
        return [send(own, own, X.at[k, (z + 8 - d) % 8, xh, y, rs], at(dz=d)) for d in (4, 3, 5, 2, 6, 1, 7)]

    def order_x(k, rs, when):
        w = {}

        def to_x(dy):
            own = X.at[k, :, xh, (y + 4 - dy) % 4, rs]
            pending[k].append(send(own, own, X.at[k, :, 1 - xh, (y + 4 - dy) % 4, rs], at(dx=1)))

        def first():
            w["z"] = z_direct(k, rs)

        def second():
            wait_all(w["z"])
            own = X.at[k, :, xh, y, rs]
            w["y"] = [send(own, own, X.at[k, :, xh, (y + 4 - d) % 4, rs], at(dy=d)) for d in (1, 3, 2)]
            to_x(0)

        def third():
            for n, d in enumerate((1, 3, 2)):
                w["y"][n]()
                to_x(d)

        for t, step in zip(when, (first, second, third)):
            event(t, step)

    def shared_bin(rs, when, x_first):
        w = {}
        swapper = (b, z * 8 + xh * 4 + swap_y)
        facing = (b, z * 8 + xh * 4 + 3 - y)
        both, far = pl.ds(first_y, 2), pl.ds(2 - first_y, 2)

        def over_z(line):
            own = X.at[0, z, xh, line, rs]
            return {d: send(own, own, X.at[0, (z + 8 - d) % 8, xh, line, rs], at(dz=d)) for d in (2, 6, 1, 7)}

        w["x"], w["facing"] = [], []

        def spread(d):
            own = X.at[0, (z + 8 - d) % 8, xh, both, rs]
            w["x"].append(send(own, own, X.at[0, (z + 8 - d) % 8, 1 - xh, both, rs], at(dx=1)))
            w["facing"].append(send(own, own, X.at[0, (z + 8 - d) % 8, xh, far, rs], facing))

        def first():
            w["pair"] = send(given.at[rs], X.at[0, z, xh, y, rs], X.at[0, z, xh, swap_y, rs], swapper)
            w["own"] = over_z(y)

        def second():
            w["pair"]()
            w["other"] = over_z(swap_y)
            spread(0)

        def pass_on(d, onward, part):
            block = X.at[0, (z + 8 - d) % 8, xh, both, rs]
            w[3 if onward == 1 else 5] = send(
                block, block, X.at[0, (z + 8 - onward - d) % 8, xh, both, rs], at(dz=onward)
            )
            block = X.at[0, (z + 8 - d) % 8, xh, both, part]
            w.setdefault(4, []).append(send(block, block, X.at[0, (z + 4) % 8, xh, both, part], at(dz=d)))

        def third(d):
            w["own"][d]()
            w["other"][d]()
            if d == 2:
                pass_on(2, 1, pl.ds(rs.start, rs.size // 2))
            if d == 6:
                pass_on(6, 7, pl.ds(rs.start + rs.size // 2, rs.size // 2))
            spread(d)

        def relayed():
            for d in (3, 5):
                w[d]()
                spread(d)
            wait_all(w[4])
            spread(4)

        def fourth():
            if x_first:
                wait_all(w["x"])
                own = X.at[0, :, 1 - xh, both, rs]
                pending[0].append(send(own, own, X.at[0, :, 1 - xh, far, rs], facing))
                pending[0].extend(w["facing"])
            else:
                wait_all(w["facing"])
                own = X.at[0, :, xh, far, rs]
                pending[0].append(send(own, own, X.at[0, :, 1 - xh, far, rs], at(dx=1)))
                pending[0].extend(w["x"])

        event(when[0], first)
        event(when[1], second)
        for n, d in enumerate((2, 6, 1, 7)):
            event(when[2] + n * when[3], functools.partial(third, d))
        event(when[5], relayed)
        event(when[4], fourth)

    def swap(n):
        quarter = pl.ds(n * 1024, 1024)
        there = T.at[1, :, :, quarter]
        swapper = (b, z * 8 + xh * 4 + swap_y)
        pending[0].append(send(foc.at[1 - mine, :, :, quarter], there, there, swapper))

    def order_z(k, rs, when):
        w = {}
        ring = {}

        def pass_on(far, d):
            line = (y + 4 - d) % 4
            if far < 4:
                if far:
                    ring[d][0]()
                h = pl.ds(0, 2) if far < 3 else pl.ds(0, 1)
                piece = X.at[k, (z + 8 - far) % 8, h, line, rs]
                up = send(piece, piece, X.at[k, (z + 7 - far) % 8, h, line, rs], at(dz=1))
                if far:
                    ring[d][1]()
                h = pl.ds(0, 2) if far < 3 else pl.ds(1, 1)
                piece = X.at[k, (z + far) % 8, h, line, rs]
                down = send(piece, piece, X.at[k, (z + far + 1) % 8, h, line, rs], at(dz=7))
                ring[d] = (up, down)
                if far == 3:
                    pending[k].extend((up, down))

        def first():
            own = X.at[k, z, xh, y, rs]
            w["x"] = send(own, own, X.at[k, z, 1 - xh, y, rs], at(dx=1))

        def second():
            w["x"]()
            own = X.at[k, z, :, y, rs]
            w["y"] = [send(own, own, X.at[k, z, :, (y + 4 - d) % 4, rs], at(dy=d)) for d in (1, 3, 2)]
            pass_on(0, 0)

        def third():
            for n, d in enumerate((1, 3, 2)):
                w["y"][n]()
                pass_on(0, d)

        def later(far):
            for d in (0, 1, 3, 2):
                pass_on(far, d)

        for t, step in zip(when, (first, second, third)):
            event(t, step)
        for far in range(1, 4):
            event(when[2 + far], functools.partial(later, far))

    side, slot = (z // 2) % 2, (z // 4) * 2 + z % 2

    def give_columns(k, own, line, local):
        base = count[0]
        count[0] += 16
        place, landed = ycol.at[k, c, slot], rsem.at[base + slot * 2 + c]
        for n, d in enumerate((4, 3, 5, 2, 6, 1, 7) if local else (4, 3, 5, 2, 6, 1, 7, 0)):
            to = ((z + d) % 8) * 8 + xh * 4 + line
            copy = pltpu.make_async_remote_copy(
                src_ref=own, dst_ref=place, send_sem=ssem.at[base + n], recv_sem=landed,
                device_id=(xl * 2 + side, to), device_id_type=MESH,
            )
            copy.start()
            sent.append(copy)
        if local:
            copy = pltpu.make_async_remote_copy(
                src_ref=own, dst_ref=place, send_sem=ssem.at[base + 8], recv_sem=landed,
                device_id=sibling, device_id_type=MESH,
            )
            pl.when(side != c)(copy.start)
            to_sibling.append((side != c, copy))
            pl.when(side == c)(pltpu.make_async_copy(own, place, landed).start)
        return base

    def take_columns(k, base):
        return [
            pltpu.make_async_copy(ycol.at[k, s, j], ycol.at[k, s, j], rsem.at[base + j * 2 + s]).wait
            for j in range(4)
            for s in range(2)
        ]

    def complex_parts(acc):
        real = acc[:64, :128] - acc[64:, 128:]
        imag = acc[:64, 128:] + acc[64:, :128]
        return jnp.concatenate([real, imag], axis=1).astype(BF16)

    others = ((1, 2), (1, 1), (1, 3), (1, 0), (0, 2), (0, 1), (0, 3))

    def done_2():
        wait_all(pending[2])
        loads[1].wait()

        def plane(i, acc):
            cols = pl.ds(pl.multiple_of(i * 512, 512), 512)
            return acc + jnp.dot(
                T[2, :, :, cols].reshape(128, 512), X[2, i].reshape(512, 256), preferred_element_type=F32
            )

        yrow[2, 0, xh, y] = complex_parts(lax.fori_loop(0, 8, plane, jnp.zeros((128, 256), F32)))
        own = yrow.at[2, 0, xh, y]
        columns[2] = take_columns(2, give_columns(2, own, y, True))
        rows[2] = [
            send(own, own, yrow.at[2, 0, (xh + dx) % 2, (y + 4 - dy) % 4], at(dx=dx, dy=dy)) for dx, dy in others
        ]

    def done_mine():
        loads[0].wait()
        wait_all(pending[0])

        def plane(i, acc):
            cols = pl.ds(pl.multiple_of(i * 512, 512), 512)
            return acc + jnp.dot(
                T[pl.ds(0, 2), :, :, cols].reshape(256, 512), X[0, i].reshape(512, 256), preferred_element_type=F32
            )

        acc = lax.fori_loop(0, 8, plane, jnp.zeros((256, 256), F32))
        yrow[mine, 0, xh, y] = complex_parts(acc[:128])
        yrow[mine, 0, xh, swap_y] = complex_parts(acc[128:])
        first_base = give_columns(mine, yrow.at[mine, 0, xh, y], y, True)
        second_base = give_columns(mine, yrow.at[mine, 0, xh, swap_y], swap_y, False)
        columns[0] = take_columns(mine, first_base) + take_columns(1 - mine, second_base)
        both = yrow.at[mine, 0, xh, pl.ds(first_y, 2)]
        rows[0] = []
        for dx, dy in others:
            from_y = (y + 4 - dy) % 4
            landing = yrow.at[1 - ((from_y + 1) // 2) % 2, 0, (xh + dx) % 2, pl.ds((from_y // 2) * 2, 2)]
            rows[0].append(send(both, both, landing, at(dx=dx, dy=dy)))

    def rows_here(k):
        wait_all(rows[k])
        shared[k] = [
            send(yrow.at[i, 0], yrow.at[i, 1], yrow.at[i, 1], sibling) for i in ((0, 1) if k == 0 else (2,))
        ]

    def operands(k):
        one, two = ycol[k, c].reshape(256, 256), ycol[k, 1 - c].reshape(256, 256)
        right = jnp.concatenate([one, two], axis=1)
        return right, jnp.concatenate([-one[:, 128:], one[:, :128], -two[:, 128:], two[:, :128]], axis=1)

    def half_tile(k, half, pair):
        left = jnp.concatenate([yrow[k, s, half].reshape(256, 256) for s in range(2)], axis=1)
        return [dot_t(left, side_by) for side_by in pair]

    def gram_mine():
        wait_all(shared[0])
        wait_all(columns[0])
        pairs = operands(0), operands(1)
        for half in range(2):
            tiles = half_tile(0, half, pairs[0]), half_tile(1, half, pairs[1])
            for part in range(2):
                G[half, part] = tiles[0][part] + tiles[1][part]

    def gram_2():
        wait_all(shared[2])
        wait_all(columns[2])
        last.extend(operands(2))

    rows, columns, shared, to_sibling, last = {}, {}, {}, [], []
    for kind, first_row, n_rows in PIECES:
        make = {"X": order_x, "Z": order_z}[kind]
        make(2, pl.ds(first_row, n_rows), WHEN[kind])
    for (first_row, n_rows), when in zip(SHARED, SHARED_WHEN):
        shared_bin(pl.ds(first_row, n_rows), when, first_row == 0)
    for n in range(4):
        event(SWAP_WHEN[n], functools.partial(swap, n))
    event(DONE_2, done_2)
    event(ROWS_2, functools.partial(rows_here, 2))
    event(GRAM_2, gram_2)
    event(DONE_M, done_mine)
    event(ROWS_M, functools.partial(rows_here, 0))
    event(GRAM_M, gram_mine)
    for e in sorted(events, key=lambda e: e[:2]):
        e[2]()

    final = []
    before_final = len(sent)
    for n, half in enumerate(((xh + 1) % 2, xh)):
        for part, term in enumerate(half_tile(2, half, last)):
            G[half, part] += term
        total = G[half] * scale
        for part in range(2):
            S[part, half] = total[:, :, part * 128 : (part + 1) * 128].reshape(2, 4, 64, 128).astype(BF16)
        dx = 1 - n
        for dl, dy in ((1, 2), (1, 1), (1, 3), (0, 2), (0, 1), (0, 3), (1, 0), (0, 0)):
            if dl or dx or dy:
                to_l, to_x, to_y = (xl + dl) % 2, (xh + dx) % 2, (y + dy) % 4
                final.append(
                    send(
                        S.at[to_l, to_x, :, to_y],
                        R.at[xl, xh, y],
                        R.at[(xl + dl) % 2, (xh + dx) % 2, (y + 4 - dy) % 4],
                        (to_l * 2 + c, z * 8 + to_x * 4 + to_y),
                    )
                )
    R[xl, xh, y] = S[xl, xh, :, y]
    for copy in sent[:before_final]:
        copy.wait_send()
    for started, copy in to_sibling:
        pl.when(started)(copy.wait_send)
    wait_all(final)
    for zi in range(2):
        for h in range(2):
            for yp in range(2):
                lanes = slice(zi * 64, zi * 64 + 64)
                pair = [
                    R[0, h, 2 * yp + o].astype(F32) + R[1, h, 2 * yp + o].astype(F32) for o in range(2)
                ]
                out[:, :, zi * 512 + h * 256 + yp * 128 : zi * 512 + h * 256 + yp * 128 + 128] = jnp.concatenate(
                    [pair[0][:, :, lanes], pair[1][:, :, lanes]], axis=2
                )
    for copy in sent[before_final:]:
        copy.wait_send()


def on_device(focusing, snapshots):
    scale = 1.0 / (12 * 128)
    return pl.pallas_call(
        functools.partial(kernel, scale),
        out_shape=jax.ShapeDtypeStruct((2, 64, 1024), F32),
        in_specs=[pl.BlockSpec(memory_space=pl.ANY)] * 2,
        out_specs=pl.BlockSpec(memory_space=pltpu.VMEM),
        scratch_shapes=[
            pltpu.VMEM((3, 2, 64, 128), BF16),
            pltpu.VMEM((3, 2, 64, 4096), BF16),
            pltpu.VMEM((64, 256), BF16),
            pltpu.VMEM((3, 8, 2, 4, 64, 256), BF16),
            pltpu.VMEM((3, 2, 2, 4, 64, 256), BF16),
            pltpu.VMEM((3, 2, 4, 64, 256), BF16),
            pltpu.VMEM((2, 2, 256, 256), F32),
            pltpu.VMEM((2, 2, 2, 4, 64, 128), BF16),
            pltpu.VMEM((2, 2, 4, 2, 64, 128), BF16),
            pltpu.SemaphoreType.DMA((4,)),
            pltpu.SemaphoreType.DMA((N_COPIES,)),
            pltpu.SemaphoreType.DMA((N_COPIES,)),
        ],
        compiler_params=pltpu.CompilerParams(
            collective_id=0, has_side_effects=True, vmem_limit_bytes=63 * 2**20
        ),
        name="focus_gram",
    )(focusing, snapshots)


def solution(mesh):
    placed = (P("bin", None, "row", None), P("bin", None, "row", None))
    return jax.shard_map(
        on_device, mesh=mesh, in_specs=placed, out_specs=P(None, "row", "bin"), check_vma=False
    )
```

```python
import functools

import jax
import jax.numpy as jnp
from jax import lax
from jax.experimental import pallas as pl
from jax.experimental.pallas import tpu as pltpu
from jax.sharding import PartitionSpec as P

MESH = pl.DeviceIdType.MESH
BF16 = jnp.bfloat16
F32 = jnp.float32

PIECES = (("Z", 0, 64),)
WHEN = {"X": (0.5, 8, 15), "Z": (0, 3, 6, 11, 16, 21)}
SHARED = ((0, 32), (32, 32))
SHARED_WHEN = ((0.1, 3.1, 5, 0.5, 12, 9), (0.2, 3.2, 6.8, 0.5, 13, 9.5))
SWAP_WHEN = (3.3, 3.4, 6.1, 6.2)
DONE_2, ROWS_2, GRAM_2 = 36, 44, 50
DONE_M, ROWS_M, GRAM_M = 30, 40, 45
TWO_STEPS = (2,)
RELAY_M, RELAY_2 = 36.5, 43
N_COPIES = 320
NEAR_FIRST = (1, 7, 2, 6, 3, 5, 4)


def dot_t(left, right):
    return lax.dot_general(left, right, (((1,), (1,)), ((), ())), preferred_element_type=F32)


def kernel(scale, foc, snap_hbm, out, snap, T, given, X, yrow, ycol, G, S, R, tsem, ssem, rsem):
    b = lax.axis_index("bin")
    row = lax.axis_index("row")
    xl, c = b // 2, b % 2
    z, xh, y = row // 8, (row // 4) % 2, row % 4
    mine = 1 - ((y + 1) // 2) % 2
    first_y = (y // 2) * 2
    swap_y = first_y * 2 + 1 - y

    def at(dz=0, dx=0, dy=0):
        return (b, ((z + dz) % 8) * 8 + ((xh + dx) % 2) * 4 + (y + dy) % 4)

    fetch = pltpu.make_async_copy(snap_hbm, snap, tsem.at[3])
    fetch.start()
    loads = [
        pltpu.make_async_copy(foc.at[mine], T.at[0], tsem.at[0]),
        pltpu.make_async_copy(foc.at[2], T.at[2], tsem.at[2]),
    ]
    for load in loads:
        load.start()

    partners = [at(dz=d) for d in range(1, 8)]
    for dl in range(2):
        for dx in range(2):
            for dy in range(4):
                if dl or dx or dy:
                    partners.append((((xl + dl) % 2) * 2 + c, z * 8 + ((xh + dx) % 2) * 4 + (y + dy) % 4))
    sibling = (xl * 2 + 1 - c, row)
    partners.append(sibling)
    barrier = pltpu.get_barrier_semaphore()
    for peer in partners:
        pl.semaphore_signal(barrier, inc=1, device_id=peer, device_id_type=MESH)

    fetch.wait()
    X[0, z, xh, y] = jnp.concatenate([snap[mine, 0], snap[mine, 1]], axis=1)
    X[2, z, xh, y] = jnp.concatenate([snap[2, 0], snap[2, 1]], axis=1)
    given[...] = jnp.concatenate([snap[1 - mine, 0], snap[1 - mine, 1]], axis=1)

    pl.semaphore_wait(barrier, len(partners))

    count = [0]
    sent = []

    def send(src, dst, landing, peer):
        i = count[0]
        count[0] += 1
        copy = pltpu.make_async_remote_copy(
            src_ref=src, dst_ref=dst, send_sem=ssem.at[i], recv_sem=rsem.at[i], device_id=peer, device_id_type=MESH
        )
        copy.start()
        sent.append(copy)
        arrival = pltpu.make_async_remote_copy(
            src_ref=landing, dst_ref=landing, send_sem=ssem.at[i], recv_sem=rsem.at[i], device_id=peer, device_id_type=MESH
        )
        return arrival.wait_recv

    def wait_all(waits):
        for w in waits:
            w()

    events = []
    pending = {0: [], 2: []}

    def event(when, step):
        events.append((when, len(events), step))

    def z_direct(k, rs):
        own = X.at[k, z, xh, y, rs]
        return [send(own, own, X.at[k, (z + 8 - d) % 8, xh, y, rs], at(dz=d)) for d in (4, 3, 5, 2, 6, 1, 7)]

    def order_x(k, rs, when):
        w = {}

        def to_x(dy):
            own = X.at[k, :, xh, (y + 4 - dy) % 4, rs]
            pending[k].append(send(own, own, X.at[k, :, 1 - xh, (y + 4 - dy) % 4, rs], at(dx=1)))

        def first():
            w["z"] = z_direct(k, rs)

        def second():
            wait_all(w["z"])
            own = X.at[k, :, xh, y, rs]
            w["y"] = [send(own, own, X.at[k, :, xh, (y + 4 - d) % 4, rs], at(dy=d)) for d in (1, 3, 2)]
            to_x(0)

        def third():
            for n, d in enumerate((1, 3, 2)):
                w["y"][n]()
                to_x(d)

        for t, step in zip(when, (first, second, third)):
            event(t, step)

    def shared_bin(rs, when, x_first):
        w = {}
        swapper = (b, z * 8 + xh * 4 + swap_y)
        facing = (b, z * 8 + xh * 4 + 3 - y)
        both, far = pl.ds(first_y, 2), pl.ds(2 - first_y, 2)

        def over_z(line):
            own = X.at[0, z, xh, line, rs]
            return {d: send(own, own, X.at[0, (z + 8 - d) % 8, xh, line, rs], at(dz=d)) for d in (2, 6, 1, 7)}

        w["x"], w["facing"] = [], []

        def spread(d):
            own = X.at[0, (z + 8 - d) % 8, xh, both, rs]
            w["x"].append(send(own, own, X.at[0, (z + 8 - d) % 8, 1 - xh, both, rs], at(dx=1)))
            w["facing"].append(send(own, own, X.at[0, (z + 8 - d) % 8, xh, far, rs], facing))

        def first():
            w["pair"] = send(given.at[rs], X.at[0, z, xh, y, rs], X.at[0, z, xh, swap_y, rs], swapper)
            w["own"] = over_z(y)

        def second():
            w["pair"]()
            w["other"] = over_z(swap_y)
            spread(0)

        def pass_on(d, onward, part):
            block = X.at[0, (z + 8 - d) % 8, xh, both, rs]
            w[3 if onward == 1 else 5] = send(
                block, block, X.at[0, (z + 8 - onward - d) % 8, xh, both, rs], at(dz=onward)
            )
            block = X.at[0, (z + 8 - d) % 8, xh, both, part]
            w.setdefault(4, []).append(send(block, block, X.at[0, (z + 4) % 8, xh, both, part], at(dz=d)))

        def third(d):
            w["own"][d]()
            w["other"][d]()
            if d == 2:
                pass_on(2, 1, pl.ds(rs.start, rs.size // 2))
            if d == 6:
                pass_on(6, 7, pl.ds(rs.start + rs.size // 2, rs.size // 2))
            spread(d)

        def relayed():
            for d in (3, 5):
                w[d]()
                spread(d)
            wait_all(w[4])
            spread(4)

        def fourth():
            if x_first:
                wait_all(w["x"])
                own = X.at[0, :, 1 - xh, both, rs]
                pending[0].append(send(own, own, X.at[0, :, 1 - xh, far, rs], facing))
                pending[0].extend(w["facing"])
            else:
                wait_all(w["facing"])
                own = X.at[0, :, xh, far, rs]
                pending[0].append(send(own, own, X.at[0, :, 1 - xh, far, rs], at(dx=1)))
                pending[0].extend(w["x"])

        event(when[0], first)
        event(when[1], second)
        for n, d in enumerate((2, 6, 1, 7)):
            event(when[2] + n * when[3], functools.partial(third, d))
        event(when[5], relayed)
        event(when[4], fourth)

    def swap(n):
        quarter = pl.ds(n * 1024, 1024)
        there = T.at[1, :, :, quarter]
        swapper = (b, z * 8 + xh * 4 + swap_y)
        pending[0].append(send(foc.at[1 - mine, :, :, quarter], there, there, swapper))

    def order_z(k, rs, when):
        w = {}
        ring = {}

        def pass_on(far, d):
            line = (y + 4 - d) % 4
            if far < 4:
                if far:
                    ring[d][0]()
                h = pl.ds(0, 2) if far < 3 else pl.ds(0, 1)
                piece = X.at[k, (z + 8 - far) % 8, h, line, rs]
                up = send(piece, piece, X.at[k, (z + 7 - far) % 8, h, line, rs], at(dz=1))
                if far:
                    ring[d][1]()
                h = pl.ds(0, 2) if far < 3 else pl.ds(1, 1)
                piece = X.at[k, (z + far) % 8, h, line, rs]
                down = send(piece, piece, X.at[k, (z + far + 1) % 8, h, line, rs], at(dz=7))
                ring[d] = (up, down)
                if far == 3:
                    pending[k].extend((up, down))

        def first():
            own = X.at[k, z, xh, y, rs]
            w["x"] = send(own, own, X.at[k, z, 1 - xh, y, rs], at(dx=1))

        def second():
            w["x"]()
            own = X.at[k, z, :, y, rs]
            w["y"] = [send(own, own, X.at[k, z, :, (y + 4 - d) % 4, rs], at(dy=d)) for d in (1, 3, 2)]
            pass_on(0, 0)

        def third():
            for n, d in enumerate((1, 3, 2)):
                w["y"][n]()
                pass_on(0, d)

        def later(far):
            for d in (0, 1, 3, 2):
                pass_on(far, d)

        for t, step in zip(when, (first, second, third)):
            event(t, step)
        for far in range(1, 4):
            event(when[2 + far], functools.partial(later, far))

    side, slot = (z // 2) % 2, (z // 4) * 2 + z % 2

    def give_columns(k, own, line, local):
        base = count[0]
        count[0] += 16
        place, landed = ycol.at[k, c, slot], rsem.at[base + slot * 2 + c]
        direct = (2, 6, 1, 7) if k is mine or k in TWO_STEPS else (4, 3, 5, 2, 6, 1, 7)
        for n, d in enumerate(direct if local else direct + (0,)):
            to = ((z + d) % 8) * 8 + xh * 4 + line
            copy = pltpu.make_async_remote_copy(
                src_ref=own, dst_ref=place, send_sem=ssem.at[base + n], recv_sem=landed,
                device_id=(xl * 2 + side, to), device_id_type=MESH,
            )
            copy.start()
            sent.append(copy)
        if local:
            copy = pltpu.make_async_remote_copy(
                src_ref=own, dst_ref=place, send_sem=ssem.at[base + 7], recv_sem=landed,
                device_id=sibling, device_id_type=MESH,
            )
            pl.when(side != c)(copy.start)
            to_sibling.append((side != c, copy))
            pl.when(side == c)(pltpu.make_async_copy(own, place, landed).start)
        return base

    near = ((((z + 6) % 8) // 4) * 2 + z % 2, (((z + 2) % 8) // 4) * 2 + z % 2)
    rest = tuple(j + 1 - 2 * (j % 2) for j in near)

    def column_wait(k, base, j, s):
        return pltpu.make_async_copy(ycol.at[k, s, j], ycol.at[k, s, j], rsem.at[base + j * 2 + s]).wait

    def relay_columns(k, base):
        copies = []
        for s in range(2):
            for up, j in enumerate(near):
                for hop, part in ((1, pl.ds(0, 64)), (2, pl.ds(32 * up, 32))):
                    block = ycol.at[k, s, j, part]
                    to = ((z + 8 + (hop - 2 * hop * up)) % 8) * 8 + xh * 4 + y
                    copies.append(
                        pltpu.make_async_remote_copy(
                            src_ref=block, dst_ref=block, send_sem=ssem.at[base + 8 + len(copies)],
                            recv_sem=rsem.at[base + j * 2 + s], device_id=(b, to), device_id_type=MESH,
                        )
                    )

        def relay():
            for s in range(2):
                for up, j in enumerate(near):
                    column_wait(k, base, j, s)()
                    for copy in copies[4 * s + 2 * up : 4 * s + 2 * up + 2]:
                        copy.start()

        pl.when(side != c)(relay)
        to_sibling.extend((side != c, copy) for copy in copies)

    def take_columns(k, base, relayed):
        def take():
            for s in range(2):
                for j in rest:
                    column_wait(k, base, j, s)()

            def take_near():
                for s in range(2):
                    for j in near:
                        column_wait(k, base, j, s)()

            if relayed:
                pl.when(side == c)(take_near)
            else:
                take_near()

        return [take]

    def relay_2():
        relay_columns(2, bases[2])

    def relay_mine():
        relay_columns(mine, bases[0])
        relay_columns(1 - mine, bases[1])

    bases = {}

    def complex_parts(acc):
        real = acc[:64, :128] - acc[64:, 128:]
        imag = acc[:64, 128:] + acc[64:, :128]
        return jnp.concatenate([real, imag], axis=1).astype(BF16)

    others = ((1, 2), (1, 1), (1, 3), (1, 0), (0, 2), (0, 1), (0, 3))

    def done_2():
        wait_all(pending[2])
        loads[1].wait()

        def plane(i, acc):
            cols = pl.ds(pl.multiple_of(i * 512, 512), 512)
            return acc + jnp.dot(
                T[2, :, :, cols].reshape(128, 512), X[2, i].reshape(512, 256), preferred_element_type=F32
            )

        yrow[2, 0, xh, y] = complex_parts(lax.fori_loop(0, 8, plane, jnp.zeros((128, 256), F32)))
        own = yrow.at[2, 0, xh, y]
        bases[2] = give_columns(2, own, y, True)
        columns[2] = take_columns(2, bases[2], 2 in TWO_STEPS)
        rows[2] = [
            send(own, own, yrow.at[2, 0, (xh + dx) % 2, (y + 4 - dy) % 4], at(dx=dx, dy=dy)) for dx, dy in others
        ]

    def done_mine():
        loads[0].wait()
        wait_all(pending[0])

        def plane(i, acc):
            cols = pl.ds(pl.multiple_of(i * 512, 512), 512)
            return acc + jnp.dot(
                T[pl.ds(0, 2), :, :, cols].reshape(256, 512), X[0, i].reshape(512, 256), preferred_element_type=F32
            )

        acc = lax.fori_loop(0, 8, plane, jnp.zeros((256, 256), F32))
        yrow[mine, 0, xh, y] = complex_parts(acc[:128])
        yrow[mine, 0, xh, swap_y] = complex_parts(acc[128:])
        bases[0] = give_columns(mine, yrow.at[mine, 0, xh, y], y, True)
        bases[1] = give_columns(mine, yrow.at[mine, 0, xh, swap_y], swap_y, False)
        columns[0] = take_columns(mine, bases[0], True) + take_columns(1 - mine, bases[1], True)
        both = yrow.at[mine, 0, xh, pl.ds(first_y, 2)]
        rows[0] = []
        for dx, dy in others:
            from_y = (y + 4 - dy) % 4
            landing = yrow.at[1 - ((from_y + 1) // 2) % 2, 0, (xh + dx) % 2, pl.ds((from_y // 2) * 2, 2)]
            rows[0].append(send(both, both, landing, at(dx=dx, dy=dy)))

    def rows_here(k):
        wait_all(rows[k])
        shared[k] = [
            send(yrow.at[i, 0], yrow.at[i, 1], yrow.at[i, 1], sibling) for i in ((0, 1) if k == 0 else (2,))
        ]

    def operands(k):
        one, two = ycol[k, c].reshape(256, 256), ycol[k, 1 - c].reshape(256, 256)
        right = jnp.concatenate([one, two], axis=1)
        return right, jnp.concatenate([-one[:, 128:], one[:, :128], -two[:, 128:], two[:, :128]], axis=1)

    def half_tile(k, half, pair):
        left = jnp.concatenate([yrow[k, s, half].reshape(256, 256) for s in range(2)], axis=1)
        return [dot_t(left, side_by) for side_by in pair]

    def gram_mine():
        wait_all(shared[0])
        wait_all(columns[0])
        pairs = operands(0), operands(1)
        for half in range(2):
            tiles = half_tile(0, half, pairs[0]), half_tile(1, half, pairs[1])
            for part in range(2):
                G[half, part] = tiles[0][part] + tiles[1][part]

    def gram_2():
        wait_all(shared[2])
        wait_all(columns[2])
        last.extend(operands(2))

    rows, columns, shared, to_sibling, last = {}, {}, {}, [], []
    for kind, first_row, n_rows in PIECES:
        make = {"X": order_x, "Z": order_z}[kind]
        make(2, pl.ds(first_row, n_rows), WHEN[kind])
    for (first_row, n_rows), when in zip(SHARED, SHARED_WHEN):
        shared_bin(pl.ds(first_row, n_rows), when, first_row == 0)
    for n in range(4):
        event(SWAP_WHEN[n], functools.partial(swap, n))
    event(DONE_2, done_2)
    event(RELAY_M, relay_mine)
    if 2 in TWO_STEPS:
        event(RELAY_2, relay_2)
    event(ROWS_2, functools.partial(rows_here, 2))
    event(GRAM_2, gram_2)
    event(DONE_M, done_mine)
    event(ROWS_M, functools.partial(rows_here, 0))
    event(GRAM_M, gram_mine)
    for e in sorted(events, key=lambda e: e[:2]):
        e[2]()

    final = []
    before_final = len(sent)
    for n, half in enumerate(((xh + 1) % 2, xh)):
        for part, term in enumerate(half_tile(2, half, last)):
            G[half, part] += term
        total = G[half] * scale
        for part in range(2):
            S[part, half] = total[:, :, part * 128 : (part + 1) * 128].reshape(2, 4, 64, 128).astype(BF16)
        dx = 1 - n
        for dl, dy in ((1, 2), (1, 1), (1, 3), (0, 2), (0, 1), (0, 3), (1, 0), (0, 0)):
            if dl or dx or dy:
                to_l, to_x, to_y = (xl + dl) % 2, (xh + dx) % 2, (y + dy) % 4
                final.append(
                    send(
                        S.at[to_l, to_x, :, to_y],
                        R.at[xl, xh, y],
                        R.at[(xl + dl) % 2, (xh + dx) % 2, (y + 4 - dy) % 4],
                        (to_l * 2 + c, z * 8 + to_x * 4 + to_y),
                    )
                )
    R[xl, xh, y] = S[xl, xh, :, y]
    for copy in sent[:before_final]:
        copy.wait_send()
    for started, copy in to_sibling:
        pl.when(started)(copy.wait_send)
    wait_all(final)
    for zi in range(2):
        for h in range(2):
            for yp in range(2):
                lanes = slice(zi * 64, zi * 64 + 64)
                pair = [
                    R[0, h, 2 * yp + o].astype(F32) + R[1, h, 2 * yp + o].astype(F32) for o in range(2)
                ]
                out[:, :, zi * 512 + h * 256 + yp * 128 : zi * 512 + h * 256 + yp * 128 + 128] = jnp.concatenate(
                    [pair[0][:, :, lanes], pair[1][:, :, lanes]], axis=2
                )
    for copy in sent[before_final:]:
        copy.wait_send()


def on_device(focusing, snapshots):
    scale = 1.0 / (12 * 128)
    return pl.pallas_call(
        functools.partial(kernel, scale),
        out_shape=jax.ShapeDtypeStruct((2, 64, 1024), F32),
        in_specs=[pl.BlockSpec(memory_space=pl.ANY)] * 2,
        out_specs=pl.BlockSpec(memory_space=pltpu.VMEM),
        scratch_shapes=[
            pltpu.VMEM((3, 2, 64, 128), BF16),
            pltpu.VMEM((3, 2, 64, 4096), BF16),
            pltpu.VMEM((64, 256), BF16),
            pltpu.VMEM((3, 8, 2, 4, 64, 256), BF16),
            pltpu.VMEM((3, 2, 2, 4, 64, 256), BF16),
            pltpu.VMEM((3, 2, 4, 64, 256), BF16),
            pltpu.VMEM((2, 2, 256, 256), F32),
            pltpu.VMEM((2, 2, 2, 4, 64, 128), BF16),
            pltpu.VMEM((2, 2, 4, 2, 64, 128), BF16),
            pltpu.SemaphoreType.DMA((4,)),
            pltpu.SemaphoreType.DMA((N_COPIES,)),
            pltpu.SemaphoreType.DMA((N_COPIES,)),
        ],
        compiler_params=pltpu.CompilerParams(
            collective_id=0, has_side_effects=True, vmem_limit_bytes=63 * 2**20
        ),
        name="focus_gram",
    )(focusing, snapshots)


def solution(mesh):
    placed = (P("bin", None, "row", None), P("bin", None, "row", None))
    return jax.shard_map(
        on_device, mesh=mesh, in_specs=placed, out_specs=P(None, "row", "bin"), check_vma=False
    )
```

```python
import functools

import jax
import jax.numpy as jnp
from jax import lax
from jax.experimental import pallas as pl
from jax.experimental.pallas import tpu as pltpu
from jax.sharding import PartitionSpec as P

MESH = pl.DeviceIdType.MESH
BF16 = jnp.bfloat16
F32 = jnp.float32

PIECES = (("Z", 0, 64),)
WHEN = {"X": (0.5, 8, 15), "Z": (0, 3, 6, 11, 16, 21)}
SHARED = ((0, 32), (32, 32))
SHARED_WHEN = ((0.1, 3.1, 5, 0.5, 12, 9), (0.2, 3.2, 6.8, 0.5, 13, 9.5))
SWAP_WHEN = (3.3, 3.4, 6.1, 6.2)
DONE_2, ROWS_2, GRAM_2 = 36, 44, 50
DONE_M, ROWS_M, GRAM_M = 30, 40, 45
TWO_STEPS = (2,)
RELAY_M, RELAY_2 = 36.5, 43
N_COPIES = 320
NEAR_FIRST = (1, 7, 2, 6, 3, 5, 4)


def dot_t(left, right):
    return lax.dot_general(left, right, (((1,), (1,)), ((), ())), preferred_element_type=F32)


def kernel(scale, foc, snap_hbm, out, snap, T, given, X, yrow, ycol, G, S, R, tsem, ssem, rsem):
    b = lax.axis_index("bin")
    row = lax.axis_index("row")
    xl, c = b // 2, b % 2
    z, xh, y = row // 8, (row // 4) % 2, row % 4
    mine = 1 - ((y + 1) // 2) % 2
    first_y = (y // 2) * 2
    swap_y = first_y * 2 + 1 - y

    def at(dz=0, dx=0, dy=0):
        return (b, ((z + dz) % 8) * 8 + ((xh + dx) % 2) * 4 + (y + dy) % 4)

    fetch = pltpu.make_async_copy(snap_hbm, snap, tsem.at[3])
    fetch.start()
    loads = [
        pltpu.make_async_copy(foc.at[mine], T.at[0], tsem.at[0]),
        pltpu.make_async_copy(foc.at[2], T.at[2], tsem.at[2]),
    ]
    for load in loads:
        load.start()

    partners = [at(dz=d) for d in (1, 2, 6, 7)]
    for dl in range(2):
        for dx in range(2):
            for dy in range(4):
                if dl or dx or dy:
                    partners.append((((xl + dl) % 2) * 2 + c, z * 8 + ((xh + dx) % 2) * 4 + (y + dy) % 4))
    sibling = (xl * 2 + 1 - c, row)
    partners.append(sibling)
    barrier = pltpu.get_barrier_semaphore()
    for peer in partners:
        pl.semaphore_signal(barrier, inc=1, device_id=peer, device_id_type=MESH)

    fetch.wait()
    X[0, z, xh, y] = jnp.concatenate([snap[mine, 0], snap[mine, 1]], axis=1)
    X[2, z, xh, y] = jnp.concatenate([snap[2, 0], snap[2, 1]], axis=1)
    given[...] = jnp.concatenate([snap[1 - mine, 0], snap[1 - mine, 1]], axis=1)

    pl.semaphore_wait(barrier, len(partners))

    count = [0]
    sent = []

    def send(src, dst, landing, peer):
        i = count[0]
        count[0] += 1
        copy = pltpu.make_async_remote_copy(
            src_ref=src, dst_ref=dst, send_sem=ssem.at[i], recv_sem=rsem.at[i], device_id=peer, device_id_type=MESH
        )
        copy.start()
        sent.append(copy)
        arrival = pltpu.make_async_remote_copy(
            src_ref=landing, dst_ref=landing, send_sem=ssem.at[i], recv_sem=rsem.at[i], device_id=peer, device_id_type=MESH
        )
        return arrival.wait_recv

    def wait_all(waits):
        for w in waits:
            w()

    events = []
    pending = {0: [], 2: []}

    def event(when, step):
        events.append((when, len(events), step))

    def z_direct(k, rs):
        own = X.at[k, z, xh, y, rs]
        return [send(own, own, X.at[k, (z + 8 - d) % 8, xh, y, rs], at(dz=d)) for d in (4, 3, 5, 2, 6, 1, 7)]

    def order_x(k, rs, when):
        w = {}

        def to_x(dy):
            own = X.at[k, :, xh, (y + 4 - dy) % 4, rs]
            pending[k].append(send(own, own, X.at[k, :, 1 - xh, (y + 4 - dy) % 4, rs], at(dx=1)))

        def first():
            w["z"] = z_direct(k, rs)

        def second():
            wait_all(w["z"])
            own = X.at[k, :, xh, y, rs]
            w["y"] = [send(own, own, X.at[k, :, xh, (y + 4 - d) % 4, rs], at(dy=d)) for d in (1, 3, 2)]
            to_x(0)

        def third():
            for n, d in enumerate((1, 3, 2)):
                w["y"][n]()
                to_x(d)

        for t, step in zip(when, (first, second, third)):
            event(t, step)

    def shared_bin(rs, when, x_first):
        w = {}
        swapper = (b, z * 8 + xh * 4 + swap_y)
        facing = (b, z * 8 + xh * 4 + 3 - y)
        both, far = pl.ds(first_y, 2), pl.ds(2 - first_y, 2)

        def over_z(line):
            own = X.at[0, z, xh, line, rs]
            return {d: send(own, own, X.at[0, (z + 8 - d) % 8, xh, line, rs], at(dz=d)) for d in (2, 6, 1, 7)}

        w["x"], w["facing"] = [], []

        def spread(d):
            own = X.at[0, (z + 8 - d) % 8, xh, both, rs]
            w["x"].append(send(own, own, X.at[0, (z + 8 - d) % 8, 1 - xh, both, rs], at(dx=1)))
            w["facing"].append(send(own, own, X.at[0, (z + 8 - d) % 8, xh, far, rs], facing))

        def first():
            w["pair"] = send(given.at[rs], X.at[0, z, xh, y, rs], X.at[0, z, xh, swap_y, rs], swapper)
            w["own"] = over_z(y)

        def second():
            w["pair"]()
            w["other"] = over_z(swap_y)
            spread(0)

        def pass_on(d, onward, part):
            block = X.at[0, (z + 8 - d) % 8, xh, both, rs]
            w[3 if onward == 1 else 5] = send(
                block, block, X.at[0, (z + 8 - onward - d) % 8, xh, both, rs], at(dz=onward)
            )
            block = X.at[0, (z + 8 - d) % 8, xh, both, part]
            w.setdefault(4, []).append(send(block, block, X.at[0, (z + 4) % 8, xh, both, part], at(dz=d)))

        def third(d):
            w["own"][d]()
            w["other"][d]()
            if d == 2:
                pass_on(2, 1, pl.ds(rs.start, rs.size // 2))
            if d == 6:
                pass_on(6, 7, pl.ds(rs.start + rs.size // 2, rs.size // 2))
            spread(d)

        def relayed():
            for d in (3, 5):
                w[d]()
                spread(d)
            wait_all(w[4])
            spread(4)

        def fourth():
            if x_first:
                wait_all(w["x"])
                own = X.at[0, :, 1 - xh, both, rs]
                pending[0].append(send(own, own, X.at[0, :, 1 - xh, far, rs], facing))
                pending[0].extend(w["facing"])
            else:
                wait_all(w["facing"])
                own = X.at[0, :, xh, far, rs]
                pending[0].append(send(own, own, X.at[0, :, 1 - xh, far, rs], at(dx=1)))
                pending[0].extend(w["x"])

        event(when[0], first)
        event(when[1], second)
        for n, d in enumerate((2, 6, 1, 7)):
            event(when[2] + n * when[3], functools.partial(third, d))
        event(when[5], relayed)
        event(when[4], fourth)

    def swap(n):
        quarter = pl.ds(n * 1024, 1024)
        there = T.at[1, :, :, quarter]
        swapper = (b, z * 8 + xh * 4 + swap_y)
        pending[0].append(send(foc.at[1 - mine, :, :, quarter], there, there, swapper))

    def order_z(k, rs, when):
        w = {}
        ring = {}

        def pass_on(far, d):
            line = (y + 4 - d) % 4
            if far < 4:
                if far:
                    ring[d][0]()
                h = pl.ds(0, 2) if far < 3 else pl.ds(0, 1)
                piece = X.at[k, (z + 8 - far) % 8, h, line, rs]
                up = send(piece, piece, X.at[k, (z + 7 - far) % 8, h, line, rs], at(dz=1))
                if far:
                    ring[d][1]()
                h = pl.ds(0, 2) if far < 3 else pl.ds(1, 1)
                piece = X.at[k, (z + far) % 8, h, line, rs]
                down = send(piece, piece, X.at[k, (z + far + 1) % 8, h, line, rs], at(dz=7))
                ring[d] = (up, down)
                if far == 3:
                    pending[k].extend((up, down))

        def first():
            own = X.at[k, z, xh, y, rs]
            w["x"] = send(own, own, X.at[k, z, 1 - xh, y, rs], at(dx=1))

        def second():
            w["x"]()
            own = X.at[k, z, :, y, rs]
            w["y"] = [send(own, own, X.at[k, z, :, (y + 4 - d) % 4, rs], at(dy=d)) for d in (1, 3, 2)]
            pass_on(0, 0)

        def third():
            for n, d in enumerate((1, 3, 2)):
                w["y"][n]()
                pass_on(0, d)

        def later(far):
            for d in (0, 1, 3, 2):
                pass_on(far, d)

        for t, step in zip(when, (first, second, third)):
            event(t, step)
        for far in range(1, 4):
            event(when[2 + far], functools.partial(later, far))

    side, slot = (z // 2) % 2, (z // 4) * 2 + z % 2

    def give_columns(k, own, line, local):
        base = count[0]
        count[0] += 16
        place, landed = ycol.at[k, c, slot], rsem.at[base + slot * 2 + c]
        direct = (2, 6, 1, 7) if k is mine or k in TWO_STEPS else (4, 3, 5, 2, 6, 1, 7)
        for n, d in enumerate(direct if local else direct + (0,)):
            to = ((z + d) % 8) * 8 + xh * 4 + line
            copy = pltpu.make_async_remote_copy(
                src_ref=own, dst_ref=place, send_sem=ssem.at[base + n], recv_sem=landed,
                device_id=(xl * 2 + side, to), device_id_type=MESH,
            )
            copy.start()
            sent.append(copy)
        if local:
            copy = pltpu.make_async_remote_copy(
                src_ref=own, dst_ref=place, send_sem=ssem.at[base + 7], recv_sem=landed,
                device_id=sibling, device_id_type=MESH,
            )
            pl.when(side != c)(copy.start)
            to_sibling.append((side != c, copy))
            pl.when(side == c)(pltpu.make_async_copy(own, place, landed).start)
        return base

    near = ((((z + 6) % 8) // 4) * 2 + z % 2, (((z + 2) % 8) // 4) * 2 + z % 2)
    rest = tuple(j + 1 - 2 * (j % 2) for j in near)

    def column_wait(k, base, j, s):
        return pltpu.make_async_copy(ycol.at[k, s, j], ycol.at[k, s, j], rsem.at[base + j * 2 + s]).wait

    def relay_columns(k, base):
        copies = []
        for s in range(2):
            for up, j in enumerate(near):
                for hop, part in ((1, pl.ds(0, 64)), (2, pl.ds(32 * up, 32))):
                    block = ycol.at[k, s, j, part]
                    to = ((z + 8 + (hop - 2 * hop * up)) % 8) * 8 + xh * 4 + y
                    copies.append(
                        pltpu.make_async_remote_copy(
                            src_ref=block, dst_ref=block, send_sem=ssem.at[base + 8 + len(copies)],
                            recv_sem=rsem.at[base + j * 2 + s], device_id=(b, to), device_id_type=MESH,
                        )
                    )

        def relay():
            for s in range(2):
                for up, j in enumerate(near):
                    column_wait(k, base, j, s)()
                    for copy in copies[4 * s + 2 * up : 4 * s + 2 * up + 2]:
                        copy.start()

        pl.when(side != c)(relay)
        to_sibling.extend((side != c, copy) for copy in copies)

    def take_columns(k, base, relayed):
        def take():
            for s in range(2):
                for j in rest:
                    column_wait(k, base, j, s)()

            def take_near():
                for s in range(2):
                    for j in near:
                        column_wait(k, base, j, s)()

            if relayed:
                pl.when(side == c)(take_near)
            else:
                take_near()

        return [take]

    def relay_2():
        relay_columns(2, bases[2])

    def relay_mine():
        relay_columns(mine, bases[0])
        relay_columns(1 - mine, bases[1])

    bases = {}

    def complex_parts(acc):
        real = acc[:64, :128] - acc[64:, 128:]
        imag = acc[:64, 128:] + acc[64:, :128]
        return jnp.concatenate([real, imag], axis=1).astype(BF16)

    others = ((1, 2), (1, 1), (1, 3), (1, 0), (0, 2), (0, 1), (0, 3))

    def done_2():
        wait_all(pending[2])
        loads[1].wait()

        def plane(i, acc):
            cols = pl.ds(pl.multiple_of(i * 512, 512), 512)
            return acc + jnp.dot(
                T[2, :, :, cols].reshape(128, 512), X[2, i].reshape(512, 256), preferred_element_type=F32
            )

        yrow[2, 0, xh, y] = complex_parts(lax.fori_loop(0, 8, plane, jnp.zeros((128, 256), F32)))
        own = yrow.at[2, 0, xh, y]
        bases[2] = give_columns(2, own, y, True)
        columns[2] = take_columns(2, bases[2], 2 in TWO_STEPS)
        rows[2] = [
            send(own, own, yrow.at[2, 0, (xh + dx) % 2, (y + 4 - dy) % 4], at(dx=dx, dy=dy)) for dx, dy in others
        ]

    def done_mine():
        loads[0].wait()
        wait_all(pending[0])

        def plane(i, acc):
            cols = pl.ds(pl.multiple_of(i * 512, 512), 512)
            return acc + jnp.dot(
                T[pl.ds(0, 2), :, :, cols].reshape(256, 512), X[0, i].reshape(512, 256), preferred_element_type=F32
            )

        acc = lax.fori_loop(0, 8, plane, jnp.zeros((256, 256), F32))
        yrow[mine, 0, xh, y] = complex_parts(acc[:128])
        yrow[mine, 0, xh, swap_y] = complex_parts(acc[128:])
        bases[0] = give_columns(mine, yrow.at[mine, 0, xh, y], y, True)
        bases[1] = give_columns(mine, yrow.at[mine, 0, xh, swap_y], swap_y, False)
        columns[0] = take_columns(mine, bases[0], True) + take_columns(1 - mine, bases[1], True)
        both = yrow.at[mine, 0, xh, pl.ds(first_y, 2)]
        rows[0] = []
        for dx, dy in others:
            from_y = (y + 4 - dy) % 4
            landing = yrow.at[1 - ((from_y + 1) // 2) % 2, 0, (xh + dx) % 2, pl.ds((from_y // 2) * 2, 2)]
            rows[0].append(send(both, both, landing, at(dx=dx, dy=dy)))

    def rows_here(k):
        wait_all(rows[k])
        shared[k] = [
            send(yrow.at[i, 0], yrow.at[i, 1], yrow.at[i, 1], sibling) for i in ((0, 1) if k == 0 else (2,))
        ]

    def operands(k):
        one, two = ycol[k, c].reshape(256, 256), ycol[k, 1 - c].reshape(256, 256)
        right = jnp.concatenate([one, two], axis=1)
        return right, jnp.concatenate([-one[:, 128:], one[:, :128], -two[:, 128:], two[:, :128]], axis=1)

    def half_tile(k, half, pair):
        left = jnp.concatenate([yrow[k, s, half].reshape(256, 256) for s in range(2)], axis=1)
        return [dot_t(left, side_by) for side_by in pair]

    def gram_mine():
        wait_all(shared[0])
        wait_all(columns[0])
        pairs = operands(0), operands(1)
        for half in range(2):
            tiles = half_tile(0, half, pairs[0]), half_tile(1, half, pairs[1])
            for part in range(2):
                G[half, part] = tiles[0][part] + tiles[1][part]

    def gram_2():
        wait_all(shared[2])
        wait_all(columns[2])
        last.extend(operands(2))

    rows, columns, shared, to_sibling, last = {}, {}, {}, [], []
    for kind, first_row, n_rows in PIECES:
        make = {"X": order_x, "Z": order_z}[kind]
        make(2, pl.ds(first_row, n_rows), WHEN[kind])
    for (first_row, n_rows), when in zip(SHARED, SHARED_WHEN):
        shared_bin(pl.ds(first_row, n_rows), when, first_row == 0)
    for n in range(4):
        event(SWAP_WHEN[n], functools.partial(swap, n))
    event(DONE_2, done_2)
    event(RELAY_M, relay_mine)
    if 2 in TWO_STEPS:
        event(RELAY_2, relay_2)
    event(ROWS_2, functools.partial(rows_here, 2))
    event(GRAM_2, gram_2)
    event(DONE_M, done_mine)
    event(ROWS_M, functools.partial(rows_here, 0))
    event(GRAM_M, gram_mine)
    for e in sorted(events, key=lambda e: e[:2]):
        e[2]()

    final = []
    before_final = len(sent)
    for n, half in enumerate(((xh + 1) % 2, xh)):
        for part, term in enumerate(half_tile(2, half, last)):
            G[half, part] += term
        total = G[half] * scale
        for part in range(2):
            S[part, half] = total[:, :, part * 128 : (part + 1) * 128].reshape(2, 4, 64, 128).astype(BF16)
        dx = 1 - n
        for dl, dy in ((1, 2), (1, 1), (1, 3), (0, 2), (0, 1), (0, 3), (1, 0), (0, 0)):
            if dl or dx or dy:
                to_l, to_x, to_y = (xl + dl) % 2, (xh + dx) % 2, (y + dy) % 4
                final.append(
                    send(
                        S.at[to_l, to_x, :, to_y],
                        R.at[xl, xh, y],
                        R.at[(xl + dl) % 2, (xh + dx) % 2, (y + 4 - dy) % 4],
                        (to_l * 2 + c, z * 8 + to_x * 4 + to_y),
                    )
                )
    R[xl, xh, y] = S[xl, xh, :, y]
    for copy in sent[:before_final]:
        copy.wait_send()
    for started, copy in to_sibling:
        pl.when(started)(copy.wait_send)
    wait_all(final)
    for zi in range(2):
        for h in range(2):
            for yp in range(2):
                lanes = slice(zi * 64, zi * 64 + 64)
                pair = [
                    R[0, h, 2 * yp + o].astype(F32) + R[1, h, 2 * yp + o].astype(F32) for o in range(2)
                ]
                out[:, :, zi * 512 + h * 256 + yp * 128 : zi * 512 + h * 256 + yp * 128 + 128] = jnp.concatenate(
                    [pair[0][:, :, lanes], pair[1][:, :, lanes]], axis=2
                )
    for copy in sent[before_final:]:
        copy.wait_send()


def on_device(focusing, snapshots):
    scale = 1.0 / (12 * 128)
    return pl.pallas_call(
        functools.partial(kernel, scale),
        out_shape=jax.ShapeDtypeStruct((2, 64, 1024), F32),
        in_specs=[pl.BlockSpec(memory_space=pl.ANY)] * 2,
        out_specs=pl.BlockSpec(memory_space=pltpu.VMEM),
        scratch_shapes=[
            pltpu.VMEM((3, 2, 64, 128), BF16),
            pltpu.VMEM((3, 2, 64, 4096), BF16),
            pltpu.VMEM((64, 256), BF16),
            pltpu.VMEM((3, 8, 2, 4, 64, 256), BF16),
            pltpu.VMEM((3, 2, 2, 4, 64, 256), BF16),
            pltpu.VMEM((3, 2, 4, 64, 256), BF16),
            pltpu.VMEM((2, 2, 256, 256), F32),
            pltpu.VMEM((2, 2, 2, 4, 64, 128), BF16),
            pltpu.VMEM((2, 2, 4, 2, 64, 128), BF16),
            pltpu.SemaphoreType.DMA((4,)),
            pltpu.SemaphoreType.DMA((N_COPIES,)),
            pltpu.SemaphoreType.DMA((N_COPIES,)),
        ],
        compiler_params=pltpu.CompilerParams(
            collective_id=0, has_side_effects=True, vmem_limit_bytes=63 * 2**20
        ),
        name="focus_gram",
    )(focusing, snapshots)


def solution(mesh):
    placed = (P("bin", None, "row", None), P("bin", None, "row", None))
    return jax.shard_map(
        on_device, mesh=mesh, in_specs=placed, out_specs=P(None, "row", "bin"), check_vma=False
    )
```

```python
import functools

import jax
import jax.numpy as jnp
from jax import lax
from jax.experimental import pallas as pl
from jax.experimental.pallas import tpu as pltpu
from jax.sharding import PartitionSpec as P

MESH = pl.DeviceIdType.MESH
BF16 = jnp.bfloat16
F32 = jnp.float32

PIECES = (("Z", 0, 64),)
WHEN = {"X": (0.5, 8, 15), "Z": (0, 3, 6, 11, 16, 21)}
SHARED = ((0, 32), (32, 32))
SHARED_WHEN = ((0.1, 3.1, 5, 0.5, 12, 9), (0.2, 3.2, 6.8, 0.5, 13, 9.5))
SWAP_WHEN = (3.3, 3.4, 6.1, 6.2)
DONE_2, ROWS_2, GRAM_2 = 36, 44, 50
DONE_M, ROWS_M, GRAM_M = 30, 40, 45
TWO_STEPS = (2,)
RELAY_M, RELAY_2 = 36.5, 43
N_COPIES = 320
NEAR_FIRST = (1, 7, 2, 6, 3, 5, 4)


def dot_t(left, right):
    return lax.dot_general(left, right, (((1,), (1,)), ((), ())), preferred_element_type=F32)


def kernel(scale, foc, snap_hbm, out, snap, T, given, X, yrow, ycol, G, S, R, tsem, ssem, rsem):
    b = lax.axis_index("bin")
    row = lax.axis_index("row")
    xl, c = b // 2, b % 2
    z, xh, y = row // 8, (row // 4) % 2, row % 4
    mine = 1 - ((y + 1) // 2) % 2
    first_y = (y // 2) * 2
    swap_y = first_y * 2 + 1 - y

    def at(dz=0, dx=0, dy=0):
        return (b, ((z + dz) % 8) * 8 + ((xh + dx) % 2) * 4 + (y + dy) % 4)

    fetch = pltpu.make_async_copy(snap_hbm, snap, tsem.at[3])
    fetch.start()
    loads = [
        pltpu.make_async_copy(foc.at[mine], T.at[0], tsem.at[0]),
        pltpu.make_async_copy(foc.at[2], T.at[2], tsem.at[2]),
    ]
    for load in loads:
        load.start()

    partners = [at(dz=d) for d in (1, 2, 6, 7)]
    for dl in range(2):
        for dx in range(2):
            for dy in range(4):
                if dl or dx or dy:
                    partners.append((((xl + dl) % 2) * 2 + c, z * 8 + ((xh + dx) % 2) * 4 + (y + dy) % 4))
    sibling = (xl * 2 + 1 - c, row)
    partners.append(sibling)
    barrier = pltpu.get_barrier_semaphore()
    for peer in partners:
        pl.semaphore_signal(barrier, inc=1, device_id=peer, device_id_type=MESH)

    fetch.wait()
    X[0, z, xh, y] = jnp.concatenate([snap[mine, 0], snap[mine, 1]], axis=1)
    X[2, z, xh, y] = jnp.concatenate([snap[2, 0], snap[2, 1]], axis=1)
    given[...] = jnp.concatenate([snap[1 - mine, 0], snap[1 - mine, 1]], axis=1)

    pl.semaphore_wait(barrier, len(partners))

    count = [0]
    sent = []

    def send(src, dst, landing, peer):
        i = count[0]
        count[0] += 1
        copy = pltpu.make_async_remote_copy(
            src_ref=src, dst_ref=dst, send_sem=ssem.at[i], recv_sem=rsem.at[i], device_id=peer, device_id_type=MESH
        )
        copy.start()
        sent.append(copy)
        arrival = pltpu.make_async_remote_copy(
            src_ref=landing, dst_ref=landing, send_sem=ssem.at[i], recv_sem=rsem.at[i], device_id=peer, device_id_type=MESH
        )
        return arrival.wait_recv

    def wait_all(waits):
        for w in waits:
            w()

    events = []
    pending = {0: [], 2: []}

    def event(when, step):
        events.append((when, len(events), step))

    def z_direct(k, rs):
        own = X.at[k, z, xh, y, rs]
        return [send(own, own, X.at[k, (z + 8 - d) % 8, xh, y, rs], at(dz=d)) for d in (4, 3, 5, 2, 6, 1, 7)]

    def order_x(k, rs, when):
        w = {}

        def to_x(dy):
            own = X.at[k, :, xh, (y + 4 - dy) % 4, rs]
            pending[k].append(send(own, own, X.at[k, :, 1 - xh, (y + 4 - dy) % 4, rs], at(dx=1)))

        def first():
            w["z"] = z_direct(k, rs)

        def second():
            wait_all(w["z"])
            own = X.at[k, :, xh, y, rs]
            w["y"] = [send(own, own, X.at[k, :, xh, (y + 4 - d) % 4, rs], at(dy=d)) for d in (1, 3, 2)]
            to_x(0)

        def third():
            for n, d in enumerate((1, 3, 2)):
                w["y"][n]()
                to_x(d)

        for t, step in zip(when, (first, second, third)):
            event(t, step)

    def shared_bin(rs, when, x_first):
        w = {}
        swapper = (b, z * 8 + xh * 4 + swap_y)
        facing = (b, z * 8 + xh * 4 + 3 - y)
        both, far = pl.ds(first_y, 2), pl.ds(2 - first_y, 2)

        def over_z(line):
            own = X.at[0, z, xh, line, rs]
            return {d: send(own, own, X.at[0, (z + 8 - d) % 8, xh, line, rs], at(dz=d)) for d in (2, 6, 1, 7)}

        w["x"], w["facing"] = [], []

        def spread(d):
            own = X.at[0, (z + 8 - d) % 8, xh, both, rs]
            w["x"].append(send(own, own, X.at[0, (z + 8 - d) % 8, 1 - xh, both, rs], at(dx=1)))
            w["facing"].append(send(own, own, X.at[0, (z + 8 - d) % 8, xh, far, rs], facing))

        def first():
            w["pair"] = send(given.at[rs], X.at[0, z, xh, y, rs], X.at[0, z, xh, swap_y, rs], swapper)
            w["own"] = over_z(y)

        def second():
            w["pair"]()
            w["other"] = over_z(swap_y)
            spread(0)

        def pass_on(d, onward, part):
            block = X.at[0, (z + 8 - d) % 8, xh, both, rs]
            w[3 if onward == 1 else 5] = send(
                block, block, X.at[0, (z + 8 - onward - d) % 8, xh, both, rs], at(dz=onward)
            )
            block = X.at[0, (z + 8 - d) % 8, xh, both, part]
            w.setdefault(4, []).append(send(block, block, X.at[0, (z + 4) % 8, xh, both, part], at(dz=d)))

        def third(d):
            w["own"][d]()
            w["other"][d]()
            if d == 2:
                pass_on(2, 1, pl.ds(rs.start, rs.size // 2))
            if d == 6:
                pass_on(6, 7, pl.ds(rs.start + rs.size // 2, rs.size // 2))
            spread(d)

        def relayed():
            for d in (3, 5):
                w[d]()
                spread(d)
            wait_all(w[4])
            spread(4)

        def fourth():
            if x_first:
                wait_all(w["x"])
                own = X.at[0, :, 1 - xh, both, rs]
                pending[0].append(send(own, own, X.at[0, :, 1 - xh, far, rs], facing))
                pending[0].extend(w["facing"])
            else:
                wait_all(w["facing"])
                own = X.at[0, :, xh, far, rs]
                pending[0].append(send(own, own, X.at[0, :, 1 - xh, far, rs], at(dx=1)))
                pending[0].extend(w["x"])

        event(when[0], first)
        event(when[1], second)
        for n, d in enumerate((2, 6, 1, 7)):
            event(when[2] + n * when[3], functools.partial(third, d))
        event(when[5], relayed)
        event(when[4], fourth)

    def swap(n):
        quarter = pl.ds(n * 1024, 1024)
        there = T.at[1, :, :, quarter]
        swapper = (b, z * 8 + xh * 4 + swap_y)
        pending[0].append(send(foc.at[1 - mine, :, :, quarter], there, there, swapper))

    def order_z(k, rs, when):
        w = {}
        ring = {}

        def pass_on(far, d):
            line = (y + 4 - d) % 4
            if far < 4:
                if far:
                    ring[d][0]()
                h = pl.ds(0, 2) if far < 3 else pl.ds(0, 1)
                piece = X.at[k, (z + 8 - far) % 8, h, line, rs]
                up = send(piece, piece, X.at[k, (z + 7 - far) % 8, h, line, rs], at(dz=1))
                if far:
                    ring[d][1]()
                h = pl.ds(0, 2) if far < 3 else pl.ds(1, 1)
                piece = X.at[k, (z + far) % 8, h, line, rs]
                down = send(piece, piece, X.at[k, (z + far + 1) % 8, h, line, rs], at(dz=7))
                ring[d] = (up, down)
                if far == 3:
                    pending[k].extend((up, down))

        def first():
            own = X.at[k, z, xh, y, rs]
            w["x"] = send(own, own, X.at[k, z, 1 - xh, y, rs], at(dx=1))

        def second():
            w["x"]()
            own = X.at[k, z, :, y, rs]
            w["y"] = [send(own, own, X.at[k, z, :, (y + 4 - d) % 4, rs], at(dy=d)) for d in (1, 3, 2)]
            pass_on(0, 0)

        def third():
            for n, d in enumerate((1, 3, 2)):
                w["y"][n]()
                pass_on(0, d)

        def later(far):
            for d in (0, 1, 3, 2):
                pass_on(far, d)

        for t, step in zip(when, (first, second, third)):
            event(t, step)
        for far in range(1, 4):
            event(when[2 + far], functools.partial(later, far))

    side, slot = (z // 2) % 2, (z // 4) * 2 + z % 2

    def give_columns(k, own, line, local):
        base = count[0]
        count[0] += 16
        place, landed = ycol.at[k, c, slot], rsem.at[base + slot * 2 + c]
        direct = (2, 6, 1, 7) if k is mine or k in TWO_STEPS else (4, 3, 5, 2, 6, 1, 7)
        for n, d in enumerate(direct if local else direct + (0,)):
            to = ((z + d) % 8) * 8 + xh * 4 + line
            copy = pltpu.make_async_remote_copy(
                src_ref=own, dst_ref=place, send_sem=ssem.at[base + n], recv_sem=landed,
                device_id=(xl * 2 + side, to), device_id_type=MESH,
            )
            copy.start()
            sent.append(copy)
        if local:
            copy = pltpu.make_async_remote_copy(
                src_ref=own, dst_ref=place, send_sem=ssem.at[base + 7], recv_sem=landed,
                device_id=sibling, device_id_type=MESH,
            )
            pl.when(side != c)(copy.start)
            to_sibling.append((side != c, copy))
            pl.when(side == c)(pltpu.make_async_copy(own, place, landed).start)
        return base

    near = ((((z + 6) % 8) // 4) * 2 + z % 2, (((z + 2) % 8) // 4) * 2 + z % 2)
    rest = tuple(j + 1 - 2 * (j % 2) for j in near)

    def column_wait(k, base, j, s):
        return pltpu.make_async_copy(ycol.at[k, s, j], ycol.at[k, s, j], rsem.at[base + j * 2 + s]).wait

    def relay_columns(k, base):
        copies = []
        for s in range(2):
            for up, j in enumerate(near):
                for hop, part in ((1, pl.ds(0, 64)), (2, pl.ds(32 * up, 32))):
                    block = ycol.at[k, s, j, part]
                    to = ((z + 8 + (hop - 2 * hop * up)) % 8) * 8 + xh * 4 + y
                    copies.append(
                        pltpu.make_async_remote_copy(
                            src_ref=block, dst_ref=block, send_sem=ssem.at[base + 8 + len(copies)],
                            recv_sem=rsem.at[base + j * 2 + s], device_id=(b, to), device_id_type=MESH,
                        )
                    )

        def relay():
            for s in range(2):
                for up, j in enumerate(near):
                    column_wait(k, base, j, s)()
                    for copy in copies[4 * s + 2 * up : 4 * s + 2 * up + 2]:
                        copy.start()

        pl.when(side != c)(relay)
        to_sibling.extend((side != c, copy) for copy in copies)

    def take_columns(k, base, relayed):
        def take():
            for s in range(2):
                for j in rest:
                    column_wait(k, base, j, s)()

            def take_near():
                for s in range(2):
                    for j in near:
                        column_wait(k, base, j, s)()

            if relayed:
                pl.when(side == c)(take_near)
            else:
                take_near()

        return [take]

    def relay_2():
        relay_columns(2, bases[2])

    def relay_mine():
        relay_columns(mine, bases[0])
        relay_columns(1 - mine, bases[1])

    bases = {}

    def complex_parts(acc):
        real = acc[:64, :128] - acc[64:, 128:]
        imag = acc[:64, 128:] + acc[64:, :128]
        return jnp.concatenate([real, imag], axis=1).astype(BF16)

    others = ((1, 2), (1, 1), (1, 3), (1, 0), (0, 2), (0, 1), (0, 3))

    def done_2():
        wait_all(pending[2])
        loads[1].wait()

        def plane(i, acc):
            cols = pl.ds(pl.multiple_of(i * 512, 512), 512)
            return acc + jnp.dot(
                T[2, :, :, cols].reshape(128, 512), X[2, i].reshape(512, 256), preferred_element_type=F32
            )

        yrow[2, 0, xh, y] = complex_parts(lax.fori_loop(0, 8, plane, jnp.zeros((128, 256), F32)))
        own = yrow.at[2, 0, xh, y]
        bases[2] = give_columns(2, own, y, True)
        columns[2] = take_columns(2, bases[2], 2 in TWO_STEPS)
        rows[2] = [
            send(own, own, yrow.at[2, 0, (xh + dx) % 2, (y + 4 - dy) % 4], at(dx=dx, dy=dy)) for dx, dy in others
        ]

    def done_mine():
        loads[0].wait()
        wait_all(pending[0])

        def product(owner):
            def plane(i, acc):
                cols = pl.ds(pl.multiple_of(i * 512, 512), 512)
                return acc + jnp.dot(
                    T[owner, :, :, cols].reshape(128, 512), X[0, i].reshape(512, 256), preferred_element_type=F32
                )

            return complex_parts(lax.fori_loop(0, 8, plane, jnp.zeros((128, 256), F32)))

        yrow[mine, 0, xh, swap_y] = product(1)
        bases[1] = give_columns(mine, yrow.at[mine, 0, xh, swap_y], swap_y, False)
        yrow[mine, 0, xh, y] = product(0)
        bases[0] = give_columns(mine, yrow.at[mine, 0, xh, y], y, True)
        columns[0] = take_columns(mine, bases[0], True) + take_columns(1 - mine, bases[1], True)
        both = yrow.at[mine, 0, xh, pl.ds(first_y, 2)]
        rows[0] = []
        for dx, dy in others:
            from_y = (y + 4 - dy) % 4
            landing = yrow.at[1 - ((from_y + 1) // 2) % 2, 0, (xh + dx) % 2, pl.ds((from_y // 2) * 2, 2)]
            rows[0].append(send(both, both, landing, at(dx=dx, dy=dy)))

    def rows_here(k):
        wait_all(rows[k])
        shared[k] = [
            send(yrow.at[i, 0], yrow.at[i, 1], yrow.at[i, 1], sibling) for i in ((0, 1) if k == 0 else (2,))
        ]

    def operands(k):
        one, two = ycol[k, c].reshape(256, 256), ycol[k, 1 - c].reshape(256, 256)
        right = jnp.concatenate([one, two], axis=1)
        return right, jnp.concatenate([-one[:, 128:], one[:, :128], -two[:, 128:], two[:, :128]], axis=1)

    def half_tile(k, half, pair):
        left = jnp.concatenate([yrow[k, s, half].reshape(256, 256) for s in range(2)], axis=1)
        return [dot_t(left, side_by) for side_by in pair]

    def gram_mine():
        wait_all(shared[0])
        wait_all(columns[0])
        pairs = operands(0), operands(1)
        for half in range(2):
            tiles = half_tile(0, half, pairs[0]), half_tile(1, half, pairs[1])
            for part in range(2):
                G[half, part] = tiles[0][part] + tiles[1][part]

    def gram_2():
        wait_all(shared[2])
        wait_all(columns[2])
        last.extend(operands(2))

    rows, columns, shared, to_sibling, last = {}, {}, {}, [], []
    for kind, first_row, n_rows in PIECES:
        make = {"X": order_x, "Z": order_z}[kind]
        make(2, pl.ds(first_row, n_rows), WHEN[kind])
    for (first_row, n_rows), when in zip(SHARED, SHARED_WHEN):
        shared_bin(pl.ds(first_row, n_rows), when, first_row == 0)
    for n in range(4):
        event(SWAP_WHEN[n], functools.partial(swap, n))
    event(DONE_2, done_2)
    event(RELAY_M, relay_mine)
    if 2 in TWO_STEPS:
        event(RELAY_2, relay_2)
    event(ROWS_2, functools.partial(rows_here, 2))
    event(GRAM_2, gram_2)
    event(DONE_M, done_mine)
    event(ROWS_M, functools.partial(rows_here, 0))
    event(GRAM_M, gram_mine)
    for e in sorted(events, key=lambda e: e[:2]):
        e[2]()

    final = []
    before_final = len(sent)
    for n, half in enumerate(((xh + 1) % 2, xh)):
        for part, term in enumerate(half_tile(2, half, last)):
            G[half, part] += term
        total = G[half] * scale
        for part in range(2):
            S[part, half] = total[:, :, part * 128 : (part + 1) * 128].reshape(2, 4, 64, 128).astype(BF16)
        dx = 1 - n
        for dl, dy in ((1, 2), (1, 1), (1, 3), (0, 2), (0, 1), (0, 3), (1, 0), (0, 0)):
            if dl or dx or dy:
                to_l, to_x, to_y = (xl + dl) % 2, (xh + dx) % 2, (y + dy) % 4
                final.append(
                    send(
                        S.at[to_l, to_x, :, to_y],
                        R.at[xl, xh, y],
                        R.at[(xl + dl) % 2, (xh + dx) % 2, (y + 4 - dy) % 4],
                        (to_l * 2 + c, z * 8 + to_x * 4 + to_y),
                    )
                )
    R[xl, xh, y] = S[xl, xh, :, y]
    for copy in sent[:before_final]:
        copy.wait_send()
    for started, copy in to_sibling:
        pl.when(started)(copy.wait_send)
    wait_all(final)
    for zi in range(2):
        for h in range(2):
            for yp in range(2):
                lanes = slice(zi * 64, zi * 64 + 64)
                pair = [
                    R[0, h, 2 * yp + o].astype(F32) + R[1, h, 2 * yp + o].astype(F32) for o in range(2)
                ]
                out[:, :, zi * 512 + h * 256 + yp * 128 : zi * 512 + h * 256 + yp * 128 + 128] = jnp.concatenate(
                    [pair[0][:, :, lanes], pair[1][:, :, lanes]], axis=2
                )
    for copy in sent[before_final:]:
        copy.wait_send()


def on_device(focusing, snapshots):
    scale = 1.0 / (12 * 128)
    return pl.pallas_call(
        functools.partial(kernel, scale),
        out_shape=jax.ShapeDtypeStruct((2, 64, 1024), F32),
        in_specs=[pl.BlockSpec(memory_space=pl.ANY)] * 2,
        out_specs=pl.BlockSpec(memory_space=pltpu.VMEM),
        scratch_shapes=[
            pltpu.VMEM((3, 2, 64, 128), BF16),
            pltpu.VMEM((3, 2, 64, 4096), BF16),
            pltpu.VMEM((64, 256), BF16),
            pltpu.VMEM((3, 8, 2, 4, 64, 256), BF16),
            pltpu.VMEM((3, 2, 2, 4, 64, 256), BF16),
            pltpu.VMEM((3, 2, 4, 64, 256), BF16),
            pltpu.VMEM((2, 2, 256, 256), F32),
            pltpu.VMEM((2, 2, 2, 4, 64, 128), BF16),
            pltpu.VMEM((2, 2, 4, 2, 64, 128), BF16),
            pltpu.SemaphoreType.DMA((4,)),
            pltpu.SemaphoreType.DMA((N_COPIES,)),
            pltpu.SemaphoreType.DMA((N_COPIES,)),
        ],
        compiler_params=pltpu.CompilerParams(
            collective_id=0, has_side_effects=True, vmem_limit_bytes=63 * 2**20
        ),
        name="focus_gram",
    )(focusing, snapshots)


def solution(mesh):
    placed = (P("bin", None, "row", None), P("bin", None, "row", None))
    return jax.shard_map(
        on_device, mesh=mesh, in_specs=placed, out_specs=P(None, "row", "bin"), check_vma=False
    )
```
